512 devices in a mesh: row: 16 (over z, core), col: 32 (over x, y).
Axes of the slice: x: 4, y: 8, z: 8, core: 2. Of those that a mesh axis runs over, the one named last changes fastest.
Arguments:
- tokens: bfloat16 [256, 16384], P('col', 'row'), may hold values from -6 to 6
- cotangent: bfloat16 [256, 28672], P('row', 'col'), may hold values from -6 to 6
- weights: bfloat16 [2, 16384, 28672], P(None, 'row', 'col'), may hold values from -0.046875 to 0.046875
- adapter_down_master: float32 [2, 16384, 16], P(None, ('row', 'col')), may hold values from -0.046875 to 0.046875
- adapter_up_master: float32 [2, 16, 28672], P(None, None, ('col', 'row')), may hold values from -0.3 to 0.3
- down_first_moment: float32 [2, 16384, 16], P(None, ('row', 'col')), may hold values from -18 to 18
- down_second_moment: float32 [2, 16384, 16], P(None, ('row', 'col')), may hold values from 100 to 3000
- up_first_moment: float32 [2, 16, 28672], P(None, None, ('col', 'row')), may hold values from -2.4 to 2.4
- up_second_moment: float32 [2, 16, 28672], P(None, None, ('col', 'row')), may hold values from 1 to 50
Outputs:
- hidden: bfloat16 [256, 28672], P('row', 'col')
- token_input_gradient: bfloat16 [256, 16384], P('col', 'row')
- updated_down_factor: float32 [2, 16384, 16], P(None, ('row', 'col'))
- updated_up_factor: float32 [2, 16, 28672], P(None, None, ('col', 'row'))
- updated_down_first_moment: float32 [2, 16384, 16], P(None, ('row', 'col'))
- updated_down_second_moment: float32 [2, 16384, 16], P(None, ('row', 'col'))
- updated_up_first_moment: float32 [2, 16, 28672], P(None, None, ('col', 'row'))
- updated_up_second_moment: float32 [2, 16, 28672], P(None, None, ('col', 'row'))
The draws below stay inside these ranges and needn't reach their ends.
All inputs are finite; a program needn't handle non-finite values.
Results may differ from the reference program's by a relative error of at most 0.017.
Values may be sent and summed in bfloat16 or wider, within the bound.
A program may use at most 64 MiB of HBM per device.

```python
import math
import jax
import jax.numpy as jnp
from jax import lax

MODEL_WIDTH = 16384
HIDDEN_UNITS = 28672
ADAPTER_RANK = 16
TOKENS = 256


def block_scale(rng, shape, shards, smallest, top_value):
    gain = 1.0
    for dim, shards_of in shards:
        heights = jax.random.uniform(jax.random.fold_in(jax.random.fold_in(rng, 6), dim), (shards_of,), jnp.float32, smallest / len(shards), top_value / len(shards))
        gain = gain * jnp.repeat(jnp.exp(heights), shape[dim] // shards_of).reshape((-1,) + (1,) * (len(shape) - 1 - dim))
    return gain


def scatter_about(rng, dims, scale, most, cuts=(), held_as=jnp.bfloat16):
    entries = jax.random.normal(rng, dims, jnp.float32) * scale
    if len(cuts) > 0:
        entries = block_scale(rng, dims, cuts, -0.22, 0.18) * entries
    return jnp.clip(entries, min=-most, max=most).astype(held_as)


def setup_inputs(seed: int = 0) -> dict:
    key_of = jax.random.split(jax.random.key(seed), 10)
    return {
        "tokens": scatter_about(key_of[0], (TOKENS, MODEL_WIDTH), 1.0, 6.0, ((0, 32), (1, 16))),
        "cotangent": scatter_about(key_of[1], (TOKENS, HIDDEN_UNITS), 1.0, 6.0, ((0, 16), (1, 32))),
        "weights": scatter_about(key_of[2], (2, MODEL_WIDTH, HIDDEN_UNITS), MODEL_WIDTH ** -0.5, 0.046875, ((1, 16), (2, 32))),
        "adapter_down_master": scatter_about(key_of[3], (2, MODEL_WIDTH, ADAPTER_RANK), MODEL_WIDTH ** -0.5, 0.046875, ((1, 512),), jnp.float32),
        "adapter_up_master": scatter_about(key_of[4], (2, ADAPTER_RANK, HIDDEN_UNITS), 0.05, 0.3, ((2, 512),), jnp.float32),
        "down_first_moment": scatter_about(key_of[5], (2, MODEL_WIDTH, ADAPTER_RANK), 3.0, 18.0, ((1, 512),), jnp.float32),
        "down_second_moment": jnp.clip(jnp.exp(math.log(3000.0) - 3.4011974 * jax.random.uniform(key_of[6], (2, MODEL_WIDTH, ADAPTER_RANK), jnp.float32) ** block_scale(key_of[6], (2, MODEL_WIDTH, ADAPTER_RANK), ((1, 512),), -0.2, 0.2)), 100.0, 3000.0),
        "up_first_moment": scatter_about(key_of[7], (2, ADAPTER_RANK, HIDDEN_UNITS), 0.4, 2.4, ((2, 512),), jnp.float32),
        "up_second_moment": jnp.clip(jnp.exp(math.log(50.0) - 3.912023 * jax.random.uniform(key_of[8], (2, ADAPTER_RANK, HIDDEN_UNITS), jnp.float32) ** block_scale(key_of[8], (2, ADAPTER_RANK, HIDDEN_UNITS), ((2, 512),), -0.2, 0.2)), 1.0, 50.0),
    }


adapter_scale = 0.5
beta_one = 0.9
beta_two = 0.999
epsilon = 1e-08
learn_rate = 0.001
adam_step = 10.0
highest_precision = lax.Precision.HIGHEST

def moment_optimizer_update(param, moment, second, gradient):
    moment_new = beta_one * moment + (1.0 - beta_one) * gradient
    second_new = beta_two * second + (1.0 - beta_two) * gradient * gradient
    update = moment_new / (1.0 - beta_one ** adam_step) / (jnp.sqrt(second_new / (1.0 - beta_two ** adam_step)) + epsilon)
    return (param - learn_rate * update, moment_new, second_new)

def reference(tokens, cotangent, weights, adapter_down_master, adapter_up_master, down_first_moment, down_second_moment, up_first_moment, up_second_moment):
    single_float = jnp.float32
    down_factor_half = adapter_down_master.astype(jnp.bfloat16)
    up_factor_half = adapter_up_master.astype(jnp.bfloat16)
    token_float_rows = tokens.astype(single_float)
    low_rank = jnp.einsum('td,kdr->ktr', token_float_rows, down_factor_half.astype(single_float), precision=highest_precision)
    reduced_half_rows = low_rank.astype(jnp.bfloat16)
    gate_branch = jnp.dot(tokens, weights[0], preferred_element_type=single_float) + adapter_scale * jnp.einsum('zy,yu->zu', reduced_half_rows[0].astype(single_float), up_factor_half[0].astype(single_float), precision=highest_precision)
    up_projection = jnp.dot(tokens, weights[1], preferred_element_type=single_float) + adapter_scale * jnp.einsum('zy,yu->zu', reduced_half_rows[1].astype(single_float), up_factor_half[1].astype(single_float), precision=highest_precision)
    gate_sig = jax.nn.sigmoid(gate_branch)
    gate_silu = gate_branch * gate_sig
    hidden = (gate_silu * up_projection).astype(jnp.bfloat16)
    grad_out = cotangent.astype(single_float)
    d_gate = (grad_out * up_projection * gate_sig * (1.0 + gate_branch * (1.0 - gate_sig))).astype(jnp.bfloat16)
    d_upper = (grad_out * gate_silu).astype(jnp.bfloat16)
    gradient_both_branches = jnp.stack([d_gate, d_upper], axis=1).astype(single_float)
    adapter_factor = jnp.einsum('tkf,krf->ktr', gradient_both_branches, up_factor_half.astype(single_float), precision=highest_precision)
    dense_contribution = jnp.dot(d_gate, weights[0].T, preferred_element_type=single_float) + jnp.dot(d_upper, weights[1].T, preferred_element_type=single_float)
    adapter_contribution = jnp.einsum('ktr,kdr->td', adapter_factor, down_factor_half.astype(single_float), precision=highest_precision)
    token_input_gradient = (dense_contribution + adapter_scale * adapter_contribution).astype(jnp.bfloat16)
    down_factor_gradient = adapter_scale * jnp.einsum('up,quv->qpv', token_float_rows, adapter_factor, precision=highest_precision)
    up_factor_gradient = adapter_scale * jnp.einsum('dzv,zdh->dvh', reduced_half_rows.astype(single_float), gradient_both_branches, precision=highest_precision)
    updated_down_factor, updated_down_first_moment, updated_down_second_moment = moment_optimizer_update(adapter_down_master, down_first_moment, down_second_moment, down_factor_gradient)
    updated_up_factor, updated_up_first_moment, updated_up_second_moment = moment_optimizer_update(adapter_up_master, up_first_moment, up_second_moment, up_factor_gradient)
    return (hidden, token_input_gradient, updated_down_factor, updated_up_factor, updated_down_first_moment, updated_down_second_moment, updated_up_first_moment, updated_up_second_moment)
```

```python
import jax
import jax.numpy as jnp
from jax import lax
from jax.experimental import pallas as pl
from jax.experimental.pallas import tpu as pltpu
from jax.sharding import PartitionSpec as P

F32 = jnp.float32
BF16 = jnp.bfloat16
MESH = pl.DeviceIdType.MESH
adapter_scale = 0.5
beta_one = 0.9
beta_two = 0.999
epsilon = 1e-08
learn_rate = 0.001
adam_step = 10.0

NX, NY, NZ, NC = 4, 8, 8, 2
ROWS, COLS = NZ * NC, NX * NY
NEAR_LAST = (4, 3, 5, 2, 6, 1, 7)
NEAR_FIRST = (1, 7, 2, 6, 3, 5, 4)
NT = (((1,), (1,)), ((), ()))


def adam(param, moment, second, gradient):
    moment_new = beta_one * moment + (1.0 - beta_one) * gradient
    second_new = beta_two * second + (1.0 - beta_two) * gradient * gradient
    update = (
        moment_new
        / (1.0 - beta_one**adam_step)
        / (jnp.sqrt(second_new / (1.0 - beta_two**adam_step)) + epsilon)
    )
    return (param - learn_rate * update, moment_new, second_new)


def dot(a, b):
    return jnp.dot(a, b, preferred_element_type=F32)


def kernel(
    tok_h, cot_h, w_h, a_h, b_h, ma_h, va_h, mb_h, vb_h,
    hid_o, dx_o, pa_o, pb_o, mao_o, vao_o, mbo_o, vbo_o,
    tok, cot, w, a, b, ma, va, mb, vb,
    tblk, aw, bw, bblk, bf, bb, x, a4, s1, r1, y, s2, r2, d, s3, r3, s4, r4,
    in_sem, t_send, t_recv, b_send, b_recv, f_send, f_recv, d_send, d_recv, g_send, g_recv,
):
    row, col = lax.axis_index("row"), lax.axis_index("col")
    z, c = row // NC, row % NC
    px, py = col // NY, col % NY
    oc = 1 - c

    def at_z(off):
        return (lax.rem(z + off, NZ) * NC + c, col)

    partner = (z * NC + oc, col)

    def at_y(off):
        return (row, px * NY + lax.rem(py + off, NY))

    def at_x(off):
        return (row, lax.rem(px + off, NX) * NY + py)

    def at_row(off):
        return (lax.rem(row + off, ROWS), col)

    def remote(src, dst, send, recv, to):
        return pltpu.make_async_remote_copy(
            src_ref=src, dst_ref=dst, send_sem=send, recv_sem=recv, device_id=to, device_id_type=MESH
        )

    loads = [
        pltpu.make_async_copy(h, v, in_sem.at[i])
        for i, (h, v) in enumerate(
            [(tok_h, tok), (a_h, a), (b_h, b), (w_h, w), (cot_h, cot), (ma_h, ma), (va_h, va), (mb_h, mb), (vb_h, vb)]
        )
    ]
    for load in loads:
        load.start()

    barrier = pltpu.get_barrier_semaphore()
    greet = (
        [at_y(o) for o in range(1, NY)] + [at_x(o) for o in range(1, NX)] + [at_row(o) for o in range(1, ROWS)]
    )
    for peer in greet:
        pl.semaphore_signal(barrier, inc=1, device_id=peer, device_id_type=MESH)

    for load in loads[:3]:
        load.wait()
    t = tok[...].astype(F32)
    for k in range(2):
        for j in range(4):
            aw[:, 32 * j + 16 * k : 32 * j + 16 * k + 16] = a[k, 8 * j : 8 * j + 8, :]
    tblk[col, :, 0:512] = jnp.concatenate([t[:, :512], t[:, 512:]], axis=0).astype(BF16)
    tblk[col, :, 512:640] = jnp.concatenate([aw[...], jnp.zeros((8, 128), F32)], axis=0).astype(BF16)
    bw[...] = jnp.zeros((32, 128), F32)
    for k in range(2):
        bw[16 * k : 16 * k + 16, 0:56] = b[k]
    bblk[row] = bw[...].astype(BF16)

    pl.semaphore_wait(barrier, len(greet))

    sends = []

    def go(copy):
        copy.start()
        sends.append(copy)

    for o in NEAR_LAST:
        go(remote(tblk.at[col], tblk.at[col], t_send.at[o], t_recv.at[o], at_y(o)))

    def spread_x(yo):
        src = px * NY + lax.rem(py - yo + NY, NY)
        for o in (2, 1, 3):
            i = o * NY + yo
            go(remote(tblk.at[src], tblk.at[src], t_send.at[i], t_recv.at[i], at_x(o)))

    spread_x(0)
    for o in range(1, ROWS):
        go(remote(bblk.at[row], bblk.at[row], b_send.at[o], b_recv.at[o], at_row(o)))
    for o in NEAR_FIRST:
        remote(tblk.at[col], tblk.at[col], t_send.at[o], t_recv.at[o], at_y(o)).wait_recv()
        spread_x(o)

    for o in range(1, ROWS):
        remote(bblk.at[row], bblk.at[row], b_send.at[o], b_recv.at[o], at_row(o)).wait_recv()
    for r in range(ROWS):
        bf[:, 56 * r : 56 * r + 56] = bblk[r].astype(F32)[:, 0:56]
    bfull = bf[...].astype(BF16)
    zero = jnp.zeros((16, 896), BF16)
    for j in range(4):
        for k in range(2):
            g = 32 * j + 16 * k
            bb[g : g + 16, 896 * k : 896 * k + 896] = bfull[16 * k : 16 * k + 16]
            bb[g : g + 16, 896 * (1 - k) : 896 * (1 - k) + 896] = zero

    for yo in range(NY):
        for o in (1, 3, 2):
            i = o * NY + yo
            remote(tblk.at[col], tblk.at[col], t_send.at[i], t_recv.at[i], at_x(o)).wait_recv()

    v = tblk[...].astype(F32)
    v5 = v.reshape(NZ, NC, 2, 16, 640)
    for cc in range(NC):
        u = v5[:, cc].reshape(16, 16, 640)
        x[cc, :, 0:512] = u[:, :8, :512].reshape(128, 512).astype(BF16)
        x[cc, :, 512:1024] = u[:, 8:, :512].reshape(128, 512).astype(BF16)
    group = lax.broadcasted_iota(jnp.int32, (COLS, 4, 8, 128), 3) // 32
    which = lax.broadcasted_iota(jnp.int32, (COLS, 4, 8, 128), 1)
    arep = jnp.broadcast_to(v[:, None, :8, 512:640], (COLS, 4, 8, 128))
    a4[...] = jnp.where(group == which, arep, 0.0).reshape(1024, 128).astype(BF16)

    loads[3].wait()
    xo = x[oc]
    s1[:, :, 0:896] = dot(xo, w[0]).astype(BF16).reshape(NZ, 16, 896)
    s1[:, :, 896:1792] = dot(xo, w[1]).astype(BF16).reshape(NZ, 16, 896)
    s1[:, :, 1792:1920] = dot(xo, a4[...]).astype(BF16).reshape(NZ, 16, 128)
    core_sum = remote(s1, r1, f_send.at[0], f_recv.at[0], partner)
    go(core_sum)
    xm = x[c]
    y[:, :, 0:896] = dot(xm, w[0]).reshape(NZ, 16, 896)
    y[:, :, 896:1792] = dot(xm, w[1]).reshape(NZ, 16, 896)
    y[:, :, 1792:1920] = dot(xm, a4[...]).reshape(NZ, 16, 128)
    core_sum.wait_recv()
    for o in NEAR_LAST:
        to = lax.rem(z + o, NZ)
        s2[to] = (y[to] + r1[to].astype(F32)).astype(BF16)
        go(remote(s2.at[to], r2.at[o], f_send.at[o], f_recv.at[o], at_z(o)))
    total = y[z] + r1[z].astype(F32)
    for load in loads[4:]:
        load.wait()
    for o in NEAR_FIRST:
        remote(s2.at[z], r2.at[o], f_send.at[o], f_recv.at[o], at_z(o)).wait_recv()
        total = total + r2[o].astype(F32)

    low = total[:, 1792:]
    low = low + pltpu.roll(low, 64, 1)
    low = low + pltpu.roll(low, 32, 1)
    lane = lax.broadcasted_iota(jnp.int32, (16, 128), 1)
    low_half = jnp.where(lane < 32, low, 0.0).astype(BF16)
    both = total[:, :1792] + adapter_scale * dot(low_half, bb[...])
    gate, up = both[:, :896], both[:, 896:]
    sig = jax.nn.sigmoid(gate)
    silu = gate * sig
    grad = cot[...].astype(F32)
    hid_o[...] = (silu * up).astype(BF16)
    d[c, z, :, 0:896] = (grad * up * sig * (1.0 + gate * (1.0 - sig))).astype(BF16)
    d[c, z, :, 896:1792] = (grad * silu).astype(BF16)
    d[c, z, :, 1792:1920] = low_half

    for o in NEAR_LAST:
        go(remote(d.at[c, z], d.at[c, z], d_send.at[o], d_recv.at[o], at_z(o)))
    go(remote(d.at[c, z], d.at[c, z], d_send.at[0], d_recv.at[0], partner))
    for o in NEAR_FIRST:
        remote(d.at[c, z], d.at[c, z], d_send.at[o], d_recv.at[o], at_z(o)).wait_recv()
        src = lax.rem(z - o + NZ, NZ)
        go(remote(d.at[c, src], d.at[c, src], d_send.at[8 + o], d_recv.at[8 + o], partner))
    remote(d.at[c, z], d.at[c, z], d_send.at[0], d_recv.at[0], partner).wait_recv()
    for o in NEAR_FIRST:
        remote(d.at[c, z], d.at[c, z], d_send.at[8 + o], d_recv.at[8 + o], partner).wait_recv()

    dall = d[...].reshape(256, 1920)
    dg, du = dall[:, :896], dall[:, 896:1792]
    fac = lax.dot_general(dall[:, :1792], bb[...], NT, preferred_element_type=F32)
    fac = adapter_scale * fac
    fac_half = fac.astype(BF16)
    dx = lax.dot_general(dg, w[0], NT, preferred_element_type=F32)
    dx = dx + lax.dot_general(du, w[1], NT, preferred_element_type=F32)
    dx = dx + lax.dot_general(fac_half, a4[...], NT, preferred_element_type=F32)
    xall = x[...].reshape(256, 1024)
    ga = dot(fac.T.astype(BF16), xall).T.reshape(COLS, 4, 8, 128)
    ga = jnp.sum(jnp.where(group == which, ga, 0.0), axis=1)
    dx6 = dx.reshape(NC, NX, 2, 2, 8, 1024)
    for yy in range(NY):
        blk = dx6[(yy // 2) % 2, :, yy // 4, yy % 2]
        s3[:, yy, :, 0:512] = jnp.concatenate([blk[:, :, :512], blk[:, :, 512:]], axis=1)
    ga4 = ga.reshape(NX, NY, 8, 128)
    s3[:, :, :, 512:640] = jnp.concatenate([ga4, jnp.zeros_like(ga4)], axis=2)
    for o in (2, 1, 3):
        to = lax.rem(px + o, NX)
        s4[o] = s3[to].astype(BF16)
        go(remote(s4.at[o], r3.at[o], g_send.at[o], g_recv.at[o], at_x(o)))

    low_t = dall[:, 1792:].astype(F32).T[:32].astype(BF16)
    gb = adapter_scale * dot(low_t, dall[:, :1792])
    shift = lax.rem(896 - 56 * row, 896)
    for k in range(2):
        gk = pltpu.roll(gb[16 * k : 16 * k + 16, 896 * k : 896 * k + 896], shift, 1)[:, :56]
        pb_o[k], mbo_o[k], vbo_o[k] = adam(b[k], mb[k], vb[k], gk)

    part = s3[px]
    for o in (1, 3, 2):
        remote(s4.at[o], r3.at[o], g_send.at[o], g_recv.at[o], at_x(o)).wait_recv()
        part = part + r3[o].astype(F32)
    s3[px] = part
    s4[0] = part.astype(BF16)
    for o in NEAR_LAST:
        to = lax.rem(py + o, NY)
        go(remote(s4.at[0, to], r4.at[o], g_send.at[3 + o], g_recv.at[3 + o], at_y(o)))
    last = s3[px, py]
    for o in NEAR_FIRST:
        remote(s4.at[0, 0], r4.at[o], g_send.at[3 + o], g_recv.at[3 + o], at_y(o)).wait_recv()
        last = last + r4[o].astype(F32)
    dx_o[:, 0:512] = last[:8, :512].astype(BF16)
    dx_o[:, 512:1024] = last[8:, :512].astype(BF16)
    for k in range(2):
        for j in range(4):
            rows = slice(8 * j, 8 * j + 8)
            lanes = 512 + 32 * j + 16 * k
            gk = last[:8, lanes : lanes + 16]
            pa_o[k, rows, :], mao_o[k, rows, :], vao_o[k, rows, :] = adam(
                a[k, rows, :], ma[k, rows, :], va[k, rows, :], gk
            )
    for copy in sends:
        copy.wait_send()


def per_device(*args):
    tok, cot, w, a, b, ma, va, mb, vb = args
    outs = (
        jax.ShapeDtypeStruct(cot.shape, BF16),
        jax.ShapeDtypeStruct(tok.shape, BF16),
        jax.ShapeDtypeStruct(a.shape, F32),
        jax.ShapeDtypeStruct(b.shape, F32),
        jax.ShapeDtypeStruct(a.shape, F32),
        jax.ShapeDtypeStruct(a.shape, F32),
        jax.ShapeDtypeStruct(b.shape, F32),
        jax.ShapeDtypeStruct(b.shape, F32),
    )
    vmem, dma = pltpu.VMEM, pltpu.SemaphoreType.DMA
    return pl.pallas_call(
        kernel,
        out_shape=outs,
        in_specs=[pl.BlockSpec(memory_space=pl.ANY)] * 9,
        out_specs=[pl.BlockSpec(memory_space=pltpu.VMEM)] * 8,
        scratch_shapes=[vmem(v.shape, v.dtype) for v in args]
        + [
            vmem((COLS, 16, 640), BF16),
            vmem((8, 128), F32),
            vmem((32, 128), F32),
            vmem((ROWS, 32, 128), BF16),
            vmem((32, 896), F32),
            vmem((128, 1792), BF16),
            vmem((NC, 128, 1024), BF16),
            vmem((1024, 128), BF16),
            vmem((NZ, 16, 1920), BF16),
            vmem((NZ, 16, 1920), BF16),
            vmem((NZ, 16, 1920), F32),
            vmem((NZ, 16, 1920), BF16),
            vmem((NZ, 16, 1920), BF16),
            vmem((NC, NZ, 16, 1920), BF16),
            vmem((NX, NY, 16, 640), F32),
            vmem((NX, NY, 16, 640), BF16),
            vmem((NX, NY, 16, 640), BF16),
            vmem((NY, 16, 640), BF16),
            dma((9,)),
            dma((COLS,)), dma((COLS,)),
            dma((ROWS,)), dma((ROWS,)),
            dma((NZ,)), dma((NZ,)),
            dma((ROWS,)), dma((ROWS,)),
            dma((11,)), dma((11,)),
        ],
        compiler_params=pltpu.CompilerParams(
            collective_id=0, has_side_effects=True, vmem_limit_bytes=48 * 1024 * 1024
        ),
    )(*args)


def solution(mesh):
    placed = (
        P("col", "row"),
        P("row", "col"),
        P(None, "row", "col"),
        P(None, ("row", "col"), None),
        P(None, None, ("col", "row")),
        P(None, ("row", "col"), None),
        P(None, ("row", "col"), None),
        P(None, None, ("col", "row")),
        P(None, None, ("col", "row")),
    )
    return jax.shard_map(
        per_device,
        mesh=mesh,
        in_specs=placed,
        out_specs=(
            P("row", "col"),
            P("col", "row"),
            P(None, ("row", "col"), None),
            P(None, None, ("col", "row")),
            P(None, ("row", "col"), None),
            P(None, ("row", "col"), None),
            P(None, None, ("col", "row")),
            P(None, None, ("col", "row")),
        ),
        check_vma=False,
    )
```

```python
import jax
import jax.numpy as jnp
from jax import lax
from jax.experimental import pallas as pl
from jax.experimental.pallas import tpu as pltpu
from jax.sharding import PartitionSpec as P

F32 = jnp.float32
BF16 = jnp.bfloat16
MESH = pl.DeviceIdType.MESH
adapter_scale = 0.5
beta_one = 0.9
beta_two = 0.999
epsilon = 1e-08
learn_rate = 0.001
adam_step = 10.0

NX, NY, NZ, NC = 4, 8, 8, 2
ROWS, COLS = NZ * NC, NX * NY
HID = 896
WIDTH = (HID, HID + 128)
FAR_FIRST = (4, 3, 5, 2, 6, 1, 7)
NT = (((1,), (1,)), ((), ()))


def adam(param, moment, second, gradient):
    moment_new = beta_one * moment + (1.0 - beta_one) * gradient
    second_new = beta_two * second + (1.0 - beta_two) * gradient * gradient
    update = (
        moment_new
        / (1.0 - beta_one**adam_step)
        / (jnp.sqrt(second_new / (1.0 - beta_two**adam_step)) + epsilon)
    )
    return (param - learn_rate * update, moment_new, second_new)


def dot(a, b):
    return jnp.dot(a, b, preferred_element_type=F32)


def kernel(
    tok_h, cot_h, w_h, a_h, b_h, ma_h, va_h, mb_h, vb_h,
    hid_o, dx_o, pa_o, pb_o, mao_o, vao_o, mbo_o, vbo_o,
    tok, cot, w, a, b, ma, va, mb, vb,
    hid, dxv, pa, pb, mao, vao, mbo, vbo,
    tblk, aw, bw, bblk, bf, bb, x, af, at, yo, s1, r1, sa, ra, sb, rb, lows, lowr, hidf, d0, d1, fac,
    s3, s4, r3, s5, r5, ga3, ga4, gar, ga5, ga6,
    in_sem, out_sem, t_send, t_recv, b_send, b_recv, c_send, c_recv, a_send, a_recv, f_send, f_recv,
    l_send, l_recv, g_send, g_recv, p_send, p_recv, x_send, x_recv, y_send, y_recv, q_send, q_recv, k_send, k_recv,
):
    d = (d0, d1)
    row, col = lax.axis_index("row"), lax.axis_index("col")
    z, c = row // NC, row % NC
    px, py = col // NY, col % NY
    par = py % 2
    oc = 1 - c
    sgn = 1 - 2 * c

    def zc(off):
        return lax.rem(z + sgn * off + NZ, NZ)

    def at_z(off):
        return (zc(off) * NC + c, col)

    def at_y(off):
        return (row, px * NY + lax.rem(py + off, NY))

    def at_x(off):
        return (row, lax.rem(px + off, NX) * NY + py)

    def at_row(off):
        return (lax.rem(row + off, ROWS), col)

    partner = (z * NC + oc, col)

    def remote(src, dst, send, recv, to):
        return pltpu.make_async_remote_copy(
            src_ref=src, dst_ref=dst, send_sem=send, recv_sem=recv, device_id=to, device_id_type=MESH
        )

    sends = []

    def go(*copy):
        copy = remote(*copy)
        copy.start()
        sends.append(copy)

    loads = [
        pltpu.make_async_copy(h, v, in_sem.at[i])
        for i, (h, v) in enumerate(
            [(tok_h, tok), (a_h, a), (b_h, b), (w_h, w), (cot_h, cot), (ma_h, ma), (va_h, va), (mb_h, mb), (vb_h, vb)]
        )
    ]
    for load in loads:
        load.start()
    outs = [(hid, hid_o), (dxv, dx_o), (pa, pa_o), (pb, pb_o), (mao, mao_o), (vao, vao_o), (mbo, mbo_o), (vbo, vbo_o)]
    stores = [pltpu.make_async_copy(v, h, out_sem.at[i]) for i, (v, h) in enumerate(outs)]

    barrier = pltpu.get_barrier_semaphore()
    greet = (
        [at_y(o) for o in range(1, NY)] + [at_x(o) for o in range(1, NX)] + [at_row(o) for o in range(1, ROWS)]
    )
    for peer in greet:
        pl.semaphore_signal(barrier, inc=1, device_id=peer, device_id_type=MESH)

    def block(xx, yy):
        return tblk.at[2 * xx + yy // 4, (yy // 2) % 2, yy % 2]

    for load in loads[:3]:
        load.wait()
    t = tok[...].astype(F32)
    for k in range(2):
        for h in range(2):
            j = 2 * k + h
            aw[:, 32 * j : 32 * j + 32] = a[k, 8 * h : 8 * h + 8, :]
    own = block(px, py)
    own[:, 0:512] = jnp.concatenate([t[:, :512], t[:, 512:]], axis=0).astype(BF16)
    own[:, 512:640] = jnp.concatenate([aw[...], jnp.zeros((8, 128), F32)], axis=0).astype(BF16)
    bw[...] = jnp.zeros((32, 128), F32)
    for k in range(2):
        bw[16 * k : 16 * k + 16, 0:56] = b[k]
    bblk[row] = bw[...].astype(BF16)

    pl.semaphore_wait(barrier, len(greet))

    for o in FAR_FIRST:
        go(own, own, t_send.at[o], t_recv.at[o], at_y(o))

    def source(g, j):
        return lax.rem(jnp.where(par == g, 0, 1) + (0, 2, 6, 4)[j], NY)

    def spread_copy(g, j, o):
        src = block(px, lax.rem(py - source(g, j) + NY, NY))
        i = 3 * (4 * g + j) + o - 1
        return (src, src, t_send.at[8 + i], t_recv.at[8 + i], at_x(o))

    def spread(g, j):
        off = source(g, j)
        if j == 0:

            @pl.when(off != 0)
            def _():
                remote(own, own, t_send.at[off], t_recv.at[off], at_y(1)).wait_recv()
        else:
            remote(own, own, t_send.at[off], t_recv.at[off], at_y(1)).wait_recv()
        for o in (2, 1, 3):
            go(*spread_copy(g, j, o))

    for o in range(1, ROWS):
        go(bblk.at[row], bblk.at[row], b_send.at[o], b_recv.at[o], at_row(o))
    for j in range(4):
        spread(0, j)
    for j in range(4):
        spread(1, j)

    def take(g):
        for j in range(4):
            for o in (1, 3, 2):
                remote(*spread_copy(g, j, o)).wait_recv()
        for rel in range(2):
            u = tblk[:, oc if rel == 0 else c, g].astype(F32)
            x[g, 64 * rel : 64 * rel + 64, 0:512] = u[:, :8, :512].reshape(64, 512).astype(BF16)
            x[g, 64 * rel : 64 * rel + 64, 512:1024] = u[:, 8:, :512].reshape(64, 512).astype(BF16)

    def core_copy(g):
        return (s1.at[g], r1.at[g], c_send.at[g], c_recv.at[g], partner)

    def forward(g):
        src = x[g]
        gate, up = dot(src, w[0]), dot(src, w[1])
        other = [p[:64].reshape(NZ, 8, HID) for p in (gate, up)]
        s1[g] = jnp.concatenate(other, axis=1).astype(BF16)
        go(*core_copy(g))
        mine = [p[64:].reshape(NZ, 8, HID) for p in (gate, up)]
        yo[g] = jnp.concatenate(mine, axis=1)

    def sum_copy(g, i, to):
        return (sa.at[g, i], ra.at[g, i], a_send.at[5 * g + i], a_recv.at[5 * g + i], at_z(to))

    first = ((4, 2), (3, 1), (-3, -1), (1, 1), (-1, -1))

    def sum_first(g):
        remote(*core_copy(g)).wait_recv()
        yo[g] = yo[g] + r1[g].astype(F32)
        for i, (owner, to) in enumerate(first):
            sa[g, i] = yo[g, zc(owner)].astype(BF16)
            go(*sum_copy(g, i, to))

    def second_copy(g, i):
        return (sb.at[g, i], rb.at[g, i], f_send.at[2 * g + i], f_recv.at[2 * g + i], at_z((2, -2)[i]))

    def sum_second(g):
        remote(*sum_copy(g, 1, 1)).wait_recv()
        remote(*sum_copy(g, 0, 2)).wait_recv()
        sb[g, 0] = (yo[g, zc(2)] + ra[g, 0].astype(F32) + ra[g, 1].astype(F32)).astype(BF16)
        go(*second_copy(g, 0))
        remote(*sum_copy(g, 2, -1)).wait_recv()
        sb[g, 1] = (yo[g, zc(-2)] + ra[g, 2].astype(F32)).astype(BF16)
        go(*second_copy(g, 1))

    def low_copy(o):
        to = lax.rem(row + o, ROWS)
        rel = jnp.where(to % NC == c, 1, 0)
        return (lows.at[rel, to // NC], lowr.at[o], l_send.at[o], l_recv.at[o], (to, col))

    def low_sends():
        both = [
            lax.dot_general(x[g], at[...], NT, preferred_element_type=F32).reshape(NC, NZ, 8, 128) for g in range(2)
        ]
        lows[...] = jnp.concatenate(both, axis=2).astype(BF16)
        for o in range(1, ROWS):
            go(*low_copy(o))

    def low_total():
        total = lows[1, z].astype(F32)
        for o in range(1, ROWS):
            remote(*low_copy(o)).wait_recv()
            total = total + lowr[o].astype(F32)
        keep = lax.broadcasted_iota(jnp.int32, (16, 128), 1) < 32
        return jnp.where(keep, total, 0.0).astype(BF16)

    def pass_copy(g, off, to):
        blk = d[g].at[1, zc(-off)]
        i = 8 * g + (off + to) % 8
        return (blk, blk, g_send.at[i], g_recv.at[i], at_z(to))

    def cross(g, off):
        i = 8 * g + off % 8
        return (d[g].at[1, zc(-off)], d[g].at[0, zc(-off)], p_send.at[i], p_recv.at[i], partner)

    def activate(g, gate_low, up_low, low_half):
        for i in (3, 4):
            remote(*sum_copy(g, i, first[i][1])).wait_recv()
        for i in (0, 1):
            remote(*second_copy(g, i)).wait_recv()
        total = yo[g, z] + ra[g, 3].astype(F32) + ra[g, 4].astype(F32) + rb[g, 0].astype(F32) + rb[g, 1].astype(F32)
        gate = total[:8] + gate_low[8 * g : 8 * g + 8]
        up = total[8:] + up_low[8 * g : 8 * g + 8]
        sig = jax.nn.sigmoid(gate)
        silu = gate * sig
        grad = cot[...].astype(F32)[8 * g : 8 * g + 8]
        d_gate = grad * up * sig * (1.0 + gate * (1.0 - sig))
        d_up = grad * silu
        d[g][1, z, :, 0:HID] = jnp.concatenate([d_gate, d_up], axis=0).astype(BF16)
        if g == 1:
            d[g][1, z, :, HID:] = low_half
        for to in (2, 1, -2, -1):
            go(*pass_copy(g, 0, to))
        go(*cross(g, 0))
        hidf[8 * g : 8 * g + 8, :] = silu * up

    def pass_on(g):
        remote(*pass_copy(g, 0, 1)).wait_recv()
        go(*cross(g, 1))
        remote(*pass_copy(g, 0, -1)).wait_recv()
        go(*cross(g, -1))
        remote(*pass_copy(g, 0, 2)).wait_recv()
        go(*pass_copy(g, 2, 2))
        go(*pass_copy(g, 2, 1))
        remote(*pass_copy(g, 0, -2)).wait_recv()
        go(*pass_copy(g, -2, -1))
        go(*cross(g, 2))
        go(*cross(g, -2))

    def pass_last(g):
        remote(*pass_copy(g, 2, 1)).wait_recv()
        go(*cross(g, 3))
        remote(*pass_copy(g, -2, -1)).wait_recv()
        go(*cross(g, -3))
        remote(*pass_copy(g, 2, 2)).wait_recv()
        go(*cross(g, 4))
        for off in (0, 1, -1, 2, -2, 3, -3, 4):
            remote(*cross(g, off)).wait_recv()

    def halves(g):
        v = d[g][...].astype(F32)
        return [v[:, :, 8 * k : 8 * k + 8, :HID].reshape(128, HID).astype(BF16) for k in range(2)]

    def x_copy(g, o):
        return (s4.at[g, o - 1], r3.at[g, o - 1], x_send.at[3 * g + o - 1], x_recv.at[3 * g + o - 1], at_x(o))

    def backward(g):
        dg, du = halves(g)
        f = lax.dot_general(dg, bb[:, :HID], NT, preferred_element_type=F32)
        f = adapter_scale * (f + lax.dot_general(du, bb[:, HID:], NT, preferred_element_type=F32))
        e = lax.dot_general(dg, w[0], NT, preferred_element_type=F32)
        e = e + lax.dot_general(du, w[1], NT, preferred_element_type=F32)
        e = e + dot(f.astype(BF16), at[...])
        fac[g] = f
        e6 = e.reshape(2, NX, 2, 8, 1024)
        for rel in range(2):
            cc = oc if rel == 0 else c
            for h in range(2):
                blk = e6[rel, :, h]
                s3[g, :, 2 * h + cc] = jnp.concatenate([blk[:, :, :512], blk[:, :, 512:]], axis=1)
        for o in (2, 1, 3):
            s4[g, o - 1] = s3[g, lax.rem(px + o, NX)].astype(BF16)
            go(*x_copy(g, o))

    def y_copy(g, j):
        to = 2 * j + g
        o = lax.rem(to - py + NY, NY)
        return o, (s5.at[g, j], r5.at[o], y_send.at[g * 4 + j], y_recv.at[o], (row, px * NY + to))

    def x_finish(g):
        total = s3[g, px]
        for o in (1, 3, 2):
            remote(*x_copy(g, o)).wait_recv()
            total = total + r3[g, o - 1].astype(F32)
        s3[g, px] = total
        s5[g] = total.astype(BF16)
        for j in range(4):
            o, copy = y_copy(g, j)

            @pl.when(o != 0)
            def _():
                remote(*copy).start()

    def y_send_wait(g):
        for j in range(4):
            o, copy = y_copy(g, j)

            @pl.when(o != 0)
            def _():
                remote(*copy).wait_send()

    loads[3].wait()
    take(0)
    forward(0)

    for o in range(1, ROWS):
        remote(bblk.at[row], bblk.at[row], b_send.at[o], b_recv.at[o], at_row(o)).wait_recv()
    sum_first(0)
    for r in range(ROWS):
        bf[:, 56 * r : 56 * r + 56] = bblk[r].astype(F32)[:, 0:56]
    bfull = bf[...].astype(BF16)
    bb[...] = jnp.zeros((128, 2 * HID), BF16)
    bb[0:16, 0:HID] = bfull[0:16]
    bb[16:32, HID:] = bfull[16:32]
    at[...] = jnp.zeros((128, 1024), BF16)

    take(1)
    forward(1)

    lane = lax.broadcasted_iota(jnp.int32, (8, 128), 1) // 32

    def regroup(pieces, g):
        out = None
        for q in range(4):
            p = pieces[q]
            shift = (32 * (q - g[q])) % 128
            if shift:
                p = pltpu.roll(p, shift, 1)
            out = p if out is None else jnp.where(lane == q, p, out)
        return out

    v = tblk[:, :, :, :, 512:640].astype(F32).reshape(COLS, 16, 128)
    for tile in range(8):
        four = [v[4 * tile + q, :8] for q in range(4)]
        for j in range(4):
            af[8 * j : 8 * j + 8, 128 * tile : 128 * tile + 128] = regroup(four, (j,) * 4)
    at[0:32, :] = af[...].astype(BF16)
    low_sends()
    sum_first(1)
    sum_second(0)
    sum_second(1)
    loads[4].wait()
    low_half = low_total()
    gate_low = adapter_scale * dot(low_half, bb[:, :HID])
    up_low = adapter_scale * dot(low_half, bb[:, HID:])
    activate(0, gate_low, up_low, low_half)
    activate(1, gate_low, up_low, low_half)
    hid[...] = hidf[...].astype(BF16)
    stores[0].start()
    pass_on(0)
    pass_on(1)
    pass_last(0)
    backward(0)
    pass_last(1)
    backward(1)
    ga = None
    for g in range(2):
        p = dot(fac[g].T[:32].astype(BF16), x[g])
        ga = p if ga is None else ga + p
    for tile in range(8):
        four = [ga[8 * j : 8 * j + 8, 128 * tile : 128 * tile + 128] for j in range(4)]
        for q in range(4):
            yy = 4 * (tile % 2) + q
            ga3[tile // 2, yy // 2, 8 * (yy % 2) : 8 * (yy % 2) + 8, :] = regroup(four, (q,) * 4)

    def ga_x(o):
        return (ga4.at[o - 1], gar.at[o - 1], q_send.at[o - 1], q_recv.at[o - 1], at_x(o))

    for o in (2, 1, 3):
        ga4[o - 1] = ga3[lax.rem(px + o, NX)].astype(BF16)
        go(*ga_x(o))
    x_finish(0)

    low_all = d1[:, :, :, HID:].astype(F32)
    gb = [None, None]
    for g in range(2):
        low_t = low_all[:, :, 8 * g : 8 * g + 8].reshape(128, 128).T[:32].astype(BF16)
        for k, h in enumerate(halves(g)):
            p = dot(low_t, h)[16 * k : 16 * k + 16]
            gb[k] = p if g == 0 else gb[k] + p
    for load in loads[5:]:
        load.wait()
    shift = lax.rem(HID - 56 * row, HID)
    for k in range(2):
        gk = pltpu.roll(adapter_scale * gb[k], shift, 1)[:, :56]
        pb[k], mbo[k], vbo[k] = adam(b[k], mb[k], vb[k], gk)
    for i in (3, 6, 7):
        stores[i].start()
    x_finish(1)
    total = ga3[px]
    for o in (1, 3, 2):
        remote(*ga_x(o)).wait_recv()
        total = total + gar[o - 1].astype(F32)
    ga3[px] = total
    ga5[...] = total.astype(BF16)

    def ga_y(o):
        to = lax.rem(py + o, NY)
        return (ga5.at[to // 2], ga6.at[o], k_send.at[o], k_recv.at[o], (row, px * NY + to))

    for o in FAR_FIRST:
        go(*ga_y(o))
    last = s3[par, px, py // 2]
    for o in (1, 7, 2, 6, 3, 5, 4):
        remote(s5.at[0, 0], r5.at[o], y_send.at[0], y_recv.at[o], at_y(o)).wait_recv()
        last = last + r5[o].astype(F32)
    dxv[:, 0:512] = last[:8].astype(BF16)
    dxv[:, 512:1024] = last[8:].astype(BF16)
    stores[1].start()
    total = ga3[px, py // 2]
    for o in (1, 7, 2, 6, 3, 5, 4):
        remote(*ga_y(o)).wait_recv()
        total = total + ga6[o].astype(F32)
    mine = jnp.where(par == 0, total[:8], total[8:])
    for k in range(2):
        for h in range(2):
            rows = slice(8 * h, 8 * h + 8)
            lanes = 32 * (2 * k + h)
            gk = mine[:, lanes : lanes + 32]
            pa[k, rows, :], mao[k, rows, :], vao[k, rows, :] = adam(
                a[k, rows, :], ma[k, rows, :], va[k, rows, :], gk
            )
    for i in (2, 4, 5):
        stores[i].start()
    for copy in sends:
        copy.wait_send()
    y_send_wait(0)
    y_send_wait(1)
    for store in stores:
        store.wait()


def hand_over(*refs):
    ins, outs, held, (in_sem, out_sem) = refs[:8], refs[8:16], refs[16:24], refs[24:]
    loads = [pltpu.make_async_copy(ins[i], held[i], in_sem.at[i]) for i in range(8)]
    stores = [pltpu.make_async_copy(held[i], outs[i], out_sem.at[i]) for i in range(8)]
    for load in loads:
        load.start()
    for load, store in zip(loads, stores):
        load.wait()
        store.start()
    for store in stores:
        store.wait()


def per_device(tok, cot, w, a, b, ma, va, mb, vb):
    a, ma, va = (jnp.swapaxes(t, 1, 2) for t in (a, ma, va))
    args = (tok, cot, w, a, b, ma, va, mb, vb)
    outs = tuple(jax.ShapeDtypeStruct(t.shape, t.dtype) for t in (cot, tok, a, b, a, a, b, b))
    vmem, dma = pltpu.VMEM, pltpu.SemaphoreType.DMA
    res = pl.pallas_call(
        kernel,
        out_shape=outs,
        in_specs=[pl.BlockSpec(memory_space=pl.ANY)] * 9,
        out_specs=[pl.BlockSpec(memory_space=pl.ANY)] * 8,
        scratch_shapes=[vmem(t.shape, t.dtype) for t in args + outs]
        + [
            vmem((NZ, NC, 2, 16, 640), BF16),
            vmem((8, 128), F32),
            vmem((32, 128), F32),
            vmem((ROWS, 32, 128), BF16),
            vmem((32, HID), F32),
            vmem((128, 2 * HID), BF16),
            vmem((2, 128, 1024), BF16),
            vmem((32, 1024), F32),
            vmem((128, 1024), BF16),
            vmem((2, NZ, 16, HID), F32),
            vmem((2, NZ, 16, HID), BF16),
            vmem((2, NZ, 16, HID), BF16),
            vmem((2, 5, 16, HID), BF16),
            vmem((2, 5, 16, HID), BF16),
            vmem((2, 2, 16, HID), BF16),
            vmem((2, 2, 16, HID), BF16),
            vmem((NC, NZ, 16, 128), BF16),
            vmem((ROWS, 16, 128), BF16),
            vmem((16, HID), F32),
            vmem((NC, NZ, 16, WIDTH[0]), BF16),
            vmem((NC, NZ, 16, WIDTH[1]), BF16),
            vmem((2, 128, 128), F32),
            vmem((2, NX, 4, 16, 512), F32),
            vmem((2, 3, 4, 16, 512), BF16),
            vmem((2, 3, 4, 16, 512), BF16),
            vmem((2, 4, 16, 512), BF16),
            vmem((NY, 16, 512), BF16),
            vmem((NX, 4, 16, 128), F32),
            vmem((3, 4, 16, 128), BF16),
            vmem((3, 4, 16, 128), BF16),
            vmem((4, 16, 128), BF16),
            vmem((NY, 16, 128), BF16),
            dma((9,)), dma((8,)),
            dma((32,)), dma((32,)),
            dma((ROWS,)), dma((ROWS,)),
            dma((2,)), dma((2,)),
            dma((10,)), dma((10,)),
            dma((4,)), dma((4,)),
            dma((ROWS,)), dma((ROWS,)),
            dma((16,)), dma((16,)),
            dma((16,)), dma((16,)),
            dma((6,)), dma((6,)),
            dma((8,)), dma((8,)),
            dma((3,)), dma((3,)),
            dma((8,)), dma((8,)),
        ],
        compiler_params=pltpu.CompilerParams(
            collective_id=0, has_side_effects=True, vmem_limit_bytes=60 * 1024 * 1024
        ),
    )(*args)
    hid, dx, pa, pb, mao, vao, mbo, vbo = pl.pallas_call(
        hand_over,
        out_shape=outs,
        in_specs=[pl.BlockSpec(memory_space=pl.ANY)] * 8,
        out_specs=[pl.BlockSpec(memory_space=pl.ANY)] * 8,
        scratch_shapes=[vmem(t.shape, t.dtype) for t in outs] + [dma((8,)), dma((8,))],
        compiler_params=pltpu.CompilerParams(vmem_limit_bytes=60 * 1024 * 1024),
    )(*res)
    pa, mao, vao = (jnp.swapaxes(t, 1, 2) for t in (pa, mao, vao))
    return hid, dx, pa, pb, mao, vao, mbo, vbo


def solution(mesh):
    placed = (
        P("col", "row"),
        P("row", "col"),
        P(None, "row", "col"),
        P(None, ("row", "col"), None),
        P(None, None, ("col", "row")),
        P(None, ("row", "col"), None),
        P(None, ("row", "col"), None),
        P(None, None, ("col", "row")),
        P(None, None, ("col", "row")),
    )
    return jax.shard_map(
        per_device,
        mesh=mesh,
        in_specs=placed,
        out_specs=(
            P("row", "col"),
            P("col", "row"),
            P(None, ("row", "col"), None),
            P(None, None, ("col", "row")),
            P(None, ("row", "col"), None),
            P(None, ("row", "col"), None),
            P(None, None, ("col", "row")),
            P(None, None, ("col", "row")),
        ),
        check_vma=False,
    )
```

```python
import jax
import jax.numpy as jnp
from jax import lax
from jax.experimental import pallas as pl
from jax.experimental.pallas import tpu as pltpu
from jax.sharding import PartitionSpec as P

F32 = jnp.float32
BF16 = jnp.bfloat16
MESH = pl.DeviceIdType.MESH
adapter_scale = 0.5
beta_one = 0.9
beta_two = 0.999
epsilon = 1e-08
learn_rate = 0.001
adam_step = 10.0

NX, NY, NZ, NC = 4, 8, 8, 2
ROWS, COLS = NZ * NC, NX * NY
HID = 896
WIDTH = (HID, HID + 128)
FAR_FIRST = (4, 3, 5, 2, 6, 1, 7)
NT = (((1,), (1,)), ((), ()))


def adam(param, moment, second, gradient):
    moment_new = beta_one * moment + (1.0 - beta_one) * gradient
    second_new = beta_two * second + (1.0 - beta_two) * gradient * gradient
    update = (
        moment_new
        / (1.0 - beta_one**adam_step)
        / (jnp.sqrt(second_new / (1.0 - beta_two**adam_step)) + epsilon)
    )
    return (param - learn_rate * update, moment_new, second_new)


def dot(a, b):
    return jnp.dot(a, b, preferred_element_type=F32)


def kernel(
    tok_h, cot_h, w_h, a_h, b_h, ma_h, va_h, mb_h, vb_h,
    hid_o, dx_o, pa_o, pb_o, mao_o, vao_o, mbo_o, vbo_o,
    tok, cot, w, a, b, ma, va, mb, vb,
    hid, dxv, pa, pb, mao, vao, mbo, vbo,
    tblk, aw, bw, bblk, bf, bb, x, af, at, yo, s1, r1, sa, ra, sb, rb, lows, lowr, hidf, d0, d1, fac,
    s3, s4, r3, s5, r5, ga3, ga4, gar, ga5, ga6,
    in_sem, out_sem, t_send, t_recv, b_send, b_recv, c_send, c_recv, a_send, a_recv, f_send, f_recv,
    l_send, l_recv, g_send, g_recv, p_send, p_recv, x_send, x_recv, y_send, y_recv, q_send, q_recv, k_send, k_recv,
):
    d = (d0, d1)
    row, col = lax.axis_index("row"), lax.axis_index("col")
    z, c = row // NC, row % NC
    px, py = col // NY, col % NY
    par = py % 2
    oc = 1 - c
    sgn = 1 - 2 * c

    def zc(off):
        return lax.rem(z + sgn * off + NZ, NZ)

    def at_z(off):
        return (zc(off) * NC + c, col)

    def at_y(off):
        return (row, px * NY + lax.rem(py + off, NY))

    def at_x(off):
        return (row, lax.rem(px + off, NX) * NY + py)

    def at_row(off):
        return (lax.rem(row + off, ROWS), col)

    partner = (z * NC + oc, col)

    def remote(src, dst, send, recv, to):
        return pltpu.make_async_remote_copy(
            src_ref=src, dst_ref=dst, send_sem=send, recv_sem=recv, device_id=to, device_id_type=MESH
        )

    sends = []

    def go(*copy):
        copy = remote(*copy)
        copy.start()
        sends.append(copy)

    def settle(most=1000):
        for copy in sends[:most]:
            copy.wait_send()
        del sends[:most]

    barrier = pltpu.get_barrier_semaphore()
    greet = [at_y(o) for o in FAR_FIRST] + [at_x(o) for o in (2, 1, 3)] + [at_row(o) for o in range(1, ROWS)]
    for peer in greet:
        pl.semaphore_signal(barrier, inc=1, device_id=peer, device_id_type=MESH)

    loads = [
        pltpu.make_async_copy(h, v, in_sem.at[i])
        for i, (h, v) in enumerate(
            [(tok_h, tok), (a_h, a), (b_h, b), (w_h, w), (cot_h, cot), (ma_h, ma), (va_h, va), (mb_h, mb), (vb_h, vb)]
        )
    ]
    for load in loads[:3]:
        load.start()
    outs = [(hid, hid_o), (dxv, dx_o), (pa, pa_o), (pb, pb_o), (mao, mao_o), (vao, vao_o), (mbo, mbo_o), (vbo, vbo_o)]
    stores = [pltpu.make_async_copy(v, h, out_sem.at[i]) for i, (v, h) in enumerate(outs)]

    for load in loads[3:]:
        load.start()

    def block(xx, yy):
        return tblk.at[2 * xx + yy // 4, (yy // 2) % 2, yy % 2]

    for load in loads[:2]:
        load.wait()
    t = tok[...].astype(F32)
    for k in range(2):
        for h in range(2):
            j = 2 * k + h
            aw[:, 32 * j : 32 * j + 32] = a[k, 8 * h : 8 * h + 8, :]
    own = block(px, py)
    own[:, 0:512] = jnp.concatenate([t[:, :512], t[:, 512:]], axis=0).astype(BF16)
    own[:, 512:640] = jnp.concatenate([aw[...], jnp.zeros((8, 128), F32)], axis=0).astype(BF16)
    pl.semaphore_wait(barrier, len(greet))

    def blk_at(xo, yy):
        return block(lax.rem(px - xo + NX, NX), lax.rem(py - yy + NY, NY))

    def t_y(o):
        return (own, own, t_send.at[o], t_recv.at[o], at_y(o))

    def t_x(yy, xo):
        blk, i = blk_at(0, yy), 7 + 3 * yy + xo
        return (blk, blk, t_send.at[i], t_recv.at[i], at_x(xo))

    def t_near(yy, xo):
        blk, i = blk_at(xo, 0), 7 + 3 * yy + xo
        return (blk, blk, t_send.at[i], t_recv.at[i], at_y(yy))

    far = [jnp.where(par == 0, e, o) for e, o in zip((2, 6, 4, 3, 5), (3, 5, 2, 6, 4))]
    for o in far:
        go(*t_y(o))
    for o in (2, 1, 3):
        go(*t_x(0, o))
    for o in (1, 7):
        go(*t_y(o))
    loads[2].wait()
    bw[...] = jnp.zeros((32, 128), F32)
    for k in range(2):
        bw[16 * k : 16 * k + 16, 0:56] = b[k]
    bblk[z, c] = bw[...].astype(BF16)

    def b_cross():
        return (bblk.at[z, c], bblk.at[z, c], b_send.at[0], b_recv.at[0], partner)

    def b_z(o):
        return (bblk.at[z], bblk.at[z], b_send.at[o], b_recv.at[o], at_z(o))

    go(*b_cross())

    def near(xo):
        remote(*t_x(0, xo)).wait_recv()
        go(*t_near(1, xo))
        go(*t_near(7, xo))

    def spread(i):
        remote(*t_y(far[i])).wait_recv()
        for o in (2, 1, 3):
            go(*t_x(far[i], o))

    near(1)
    near(3)
    spread(0)
    spread(1)
    near(2)
    for i in (2, 3, 4):
        spread(i)
    remote(*b_cross()).wait_recv()
    for o in FAR_FIRST:
        go(*b_z(o))

    def take(g):
        @pl.when(par == g)
        def _():
            for yy in (2, 6, 4):
                for o in (1, 3, 2):
                    remote(*t_x(yy, o)).wait_recv()

        @pl.when(par != g)
        def _():
            for yy in (1, 7):
                remote(*t_y(yy)).wait_recv()
            for yy in (1, 7, 3, 5):
                for o in (1, 3, 2):
                    remote(*t_x(yy, o)).wait_recv()

        for rel in range(2):
            u = tblk[:, oc if rel == 0 else c, g].astype(F32)
            x[g, 64 * rel : 64 * rel + 64, 0:512] = u[:, :8, :512].reshape(64, 512).astype(BF16)
            x[g, 64 * rel : 64 * rel + 64, 512:1024] = u[:, 8:, :512].reshape(64, 512).astype(BF16)

    def core_copy(g):
        return (s1.at[g], r1.at[g], c_send.at[g], c_recv.at[g], partner)

    def forward(g):
        src = x[g]
        gate, up = dot(src, w[0]), dot(src, w[1])
        other = [p[:64].reshape(NZ, 8, HID) for p in (gate, up)]
        s1[g] = jnp.concatenate(other, axis=1).astype(BF16)
        go(*core_copy(g))
        mine = [p[64:].reshape(NZ, 8, HID) for p in (gate, up)]
        yo[g] = jnp.concatenate(mine, axis=1)

    def sum_copy(g, i, to):
        return (sa.at[g, i], ra.at[g, i], a_send.at[5 * g + i], a_recv.at[5 * g + i], at_z(to))

    first = ((4, 2), (3, 1), (-3, -1), (1, 1), (-1, -1))

    def sum_first(g):
        remote(*core_copy(g)).wait_recv()
        yo[g] = yo[g] + r1[g].astype(F32)
        for i, (owner, to) in enumerate(first):
            sa[g, i] = yo[g, zc(owner)].astype(BF16)
            go(*sum_copy(g, i, to))

    def second_copy(g, i):
        return (sb.at[g, i], rb.at[g, i], f_send.at[2 * g + i], f_recv.at[2 * g + i], at_z((2, -2)[i]))

    def sum_second(g):
        remote(*sum_copy(g, 1, 1)).wait_recv()
        remote(*sum_copy(g, 0, 2)).wait_recv()
        sb[g, 0] = (yo[g, zc(2)] + ra[g, 0].astype(F32) + ra[g, 1].astype(F32)).astype(BF16)
        go(*second_copy(g, 0))
        remote(*sum_copy(g, 2, -1)).wait_recv()
        sb[g, 1] = (yo[g, zc(-2)] + ra[g, 2].astype(F32)).astype(BF16)
        go(*second_copy(g, 1))

    def low_copy(o):
        to = lax.rem(row + o, ROWS)
        rel = jnp.where(to % NC == c, 1, 0)
        return (lows.at[rel, to // NC], lowr.at[o], l_send.at[o], l_recv.at[o], (to, col))

    def low_sends():
        both = [
            lax.dot_general(x[g], at[...], NT, preferred_element_type=F32).reshape(NC, NZ, 8, 128) for g in range(2)
        ]
        lows[...] = jnp.concatenate(both, axis=2).astype(BF16)
        for o in range(1, ROWS):
            go(*low_copy(o))

    def low_total():
        total = lows[1, z].astype(F32)
        for o in range(1, ROWS):
            remote(*low_copy(o)).wait_recv()
            total = total + lowr[o].astype(F32)
        keep = lax.broadcasted_iota(jnp.int32, (16, 128), 1) < 32
        return jnp.where(keep, total, 0.0).astype(BF16)

    def pass_copy(g, off, to):
        blk = d[g].at[1, zc(-off)]
        i = 8 * g + (off + to) % 8
        return (blk, blk, g_send.at[i], g_recv.at[i], at_z(to))

    def cross(g, off):
        i = 8 * g + off % 8
        return (d[g].at[1, zc(-off)], d[g].at[0, zc(-off)], p_send.at[i], p_recv.at[i], partner)

    def activate(g, gate_low, up_low, low_half):
        for i in (3, 4):
            remote(*sum_copy(g, i, first[i][1])).wait_recv()
        for i in (0, 1):
            remote(*second_copy(g, i)).wait_recv()
        total = yo[g, z] + ra[g, 3].astype(F32) + ra[g, 4].astype(F32) + rb[g, 0].astype(F32) + rb[g, 1].astype(F32)
        gate = total[:8] + gate_low[8 * g : 8 * g + 8]
        up = total[8:] + up_low[8 * g : 8 * g + 8]
        sig = jax.nn.sigmoid(gate)
        silu = gate * sig
        grad = cot[...].astype(F32)[8 * g : 8 * g + 8]
        d_gate = grad * up * sig * (1.0 + gate * (1.0 - sig))
        d_up = grad * silu
        d[g][1, z, :, 0:HID] = jnp.concatenate([d_gate, d_up], axis=0).astype(BF16)
        if g == 1:
            d[g][1, z, :, HID:] = low_half
        for to in (2, 1, -2, -1):
            go(*pass_copy(g, 0, to))
        go(*cross(g, 0))
        hidf[8 * g : 8 * g + 8, :] = silu * up

    def pass_on(g):
        remote(*pass_copy(g, 0, 1)).wait_recv()
        go(*cross(g, 1))
        remote(*pass_copy(g, 0, -1)).wait_recv()
        go(*cross(g, -1))
        remote(*pass_copy(g, 0, 2)).wait_recv()
        go(*pass_copy(g, 2, 2))
        go(*pass_copy(g, 2, 1))
        remote(*pass_copy(g, 0, -2)).wait_recv()
        go(*pass_copy(g, -2, -1))
        go(*cross(g, 2))
        go(*cross(g, -2))

    def pass_last(g):
        remote(*pass_copy(g, 2, 1)).wait_recv()
        go(*cross(g, 3))
        remote(*pass_copy(g, -2, -1)).wait_recv()
        go(*cross(g, -3))
        remote(*pass_copy(g, 2, 2)).wait_recv()
        go(*cross(g, 4))

    def crossed(g):
        for off in (0, 1, -1, 2, -2, 3, -3, 4):
            remote(*cross(g, off)).wait_recv()

    def halves(g):
        v = d[g][...].astype(F32)
        return [v[:, :, 8 * k : 8 * k + 8, :HID].reshape(128, HID).astype(BF16) for k in range(2)]

    def x_copy(g, o):
        return (s4.at[g, o - 1], r3.at[g, o - 1], x_send.at[3 * g + o - 1], x_recv.at[3 * g + o - 1], at_x(o))

    def backward(g):
        dg, du = halves(g)
        f = lax.dot_general(dg, bb[:, :HID], NT, preferred_element_type=F32)
        f = adapter_scale * (f + lax.dot_general(du, bb[:, HID:], NT, preferred_element_type=F32))
        e = lax.dot_general(dg, w[0], NT, preferred_element_type=F32)
        e = e + lax.dot_general(du, w[1], NT, preferred_element_type=F32)
        e = e + dot(f.astype(BF16), at[...])
        fac[g] = f
        e6 = e.reshape(2, NX, 2, 8, 1024)
        for rel in range(2):
            cc = oc if rel == 0 else c
            for h in range(2):
                blk = e6[rel, :, h]
                s3[g, :, 2 * h + cc] = jnp.concatenate([blk[:, :, :512], blk[:, :, 512:]], axis=1)
        for o in (2, 1, 3):
            s4[g, o - 1] = s3[g, lax.rem(px + o, NX)].astype(BF16)
            go(*x_copy(g, o))

    def y_copy(g, j):
        to = 2 * j + g
        o = lax.rem(to - py + NY, NY)
        return o, (s5.at[g, j], r5.at[o], y_send.at[g * 4 + j], y_recv.at[o], (row, px * NY + to))

    def x_finish(g):
        total = s3[g, px]
        for o in (1, 3, 2):
            remote(*x_copy(g, o)).wait_recv()
            total = total + r3[g, o - 1].astype(F32)
        s3[g, px] = total
        s5[g] = total.astype(BF16)
        for j in range(4):
            o, copy = y_copy(g, j)

            @pl.when(o != 0)
            def _():
                remote(*copy).start()

    def y_send_wait(g):
        for j in range(4):
            o, copy = y_copy(g, j)

            @pl.when(o != 0)
            def _():
                remote(*copy).wait_send()

    loads[3].wait()
    take(0)
    forward(0)

    sum_first(0)
    for o in FAR_FIRST:
        remote(*b_z(o)).wait_recv()
    for r in range(ROWS):
        bf[:, 56 * r : 56 * r + 56] = bblk[r // NC, r % NC].astype(F32)[:, 0:56]
    bfull = bf[...].astype(BF16)
    bb[...] = jnp.zeros((128, 2 * HID), BF16)
    bb[0:16, 0:HID] = bfull[0:16]
    bb[16:32, HID:] = bfull[16:32]
    at[...] = jnp.zeros((128, 1024), BF16)

    take(1)
    forward(1)

    lane = lax.broadcasted_iota(jnp.int32, (8, 128), 1) // 32

    def regroup(pieces, g):
        out = None
        for q in range(4):
            p = pieces[q]
            shift = (32 * (q - g[q])) % 128
            if shift:
                p = pltpu.roll(p, shift, 1)
            out = p if out is None else jnp.where(lane == q, p, out)
        return out

    v = tblk[:, :, :, :, 512:640].astype(F32).reshape(COLS, 16, 128)
    for tile in range(8):
        four = [v[4 * tile + q, :8] for q in range(4)]
        for j in range(4):
            af[8 * j : 8 * j + 8, 128 * tile : 128 * tile + 128] = regroup(four, (j,) * 4)
    at[0:32, :] = af[...].astype(BF16)
    low_sends()
    sum_first(1)
    sum_second(0)
    sum_second(1)
    loads[4].wait()
    low_half = low_total()
    gate_low = adapter_scale * dot(low_half, bb[:, :HID])
    up_low = adapter_scale * dot(low_half, bb[:, HID:])
    activate(0, gate_low, up_low, low_half)
    activate(1, gate_low, up_low, low_half)
    hid[...] = hidf[...].astype(BF16)
    stores[0].start()
    settle(60)
    pass_on(0)
    pass_on(1)
    pass_last(0)
    pass_last(1)
    crossed(0)
    backward(0)
    crossed(1)
    backward(1)
    ga = None
    for g in range(2):
        p = dot(fac[g].T[:32].astype(BF16), x[g])
        ga = p if ga is None else ga + p
    for tile in range(8):
        four = [ga[8 * j : 8 * j + 8, 128 * tile : 128 * tile + 128] for j in range(4)]
        for q in range(4):
            yy = 4 * (tile % 2) + q
            ga3[tile // 2, yy // 2, 8 * (yy % 2) : 8 * (yy % 2) + 8, :] = regroup(four, (q,) * 4)

    def ga_x(o):
        return (ga4.at[o - 1], gar.at[o - 1], q_send.at[o - 1], q_recv.at[o - 1], at_x(o))

    for o in (2, 1, 3):
        ga4[o - 1] = ga3[lax.rem(px + o, NX)].astype(BF16)
        go(*ga_x(o))
    x_finish(0)

    low_all = d1[:, :, :, HID:].astype(F32)
    gb = [None, None]
    for g in range(2):
        low_t = low_all[:, :, 8 * g : 8 * g + 8].reshape(128, 128).T[:32].astype(BF16)
        for k, h in enumerate(halves(g)):
            p = dot(low_t, h)[16 * k : 16 * k + 16]
            gb[k] = p if g == 0 else gb[k] + p
    for load in loads[5:]:
        load.wait()
    shift = lax.rem(HID - 56 * row, HID)
    for k in range(2):
        gk = pltpu.roll(adapter_scale * gb[k], shift, 1)[:, :56]
        pb[k], mbo[k], vbo[k] = adam(b[k], mb[k], vb[k], gk)
    for i in (3, 6, 7):
        stores[i].start()
    x_finish(1)
    total = ga3[px]
    for o in (1, 3, 2):
        remote(*ga_x(o)).wait_recv()
        total = total + gar[o - 1].astype(F32)
    ga3[px] = total
    ga5[...] = total.astype(BF16)

    def ga_y(o):
        to = lax.rem(py + o, NY)
        return (ga5.at[to // 2], ga6.at[o], k_send.at[o], k_recv.at[o], (row, px * NY + to))

    for o in FAR_FIRST:
        go(*ga_y(o))
    y_send_wait(0)
    last = s3[par, px, py // 2]
    for o in (1, 7, 2, 6, 3, 5, 4):
        remote(s5.at[0, 0], r5.at[o], y_send.at[0], y_recv.at[o], at_y(o)).wait_recv()
        last = last + r5[o].astype(F32)
    dxv[:, 0:512] = last[:8].astype(BF16)
    dxv[:, 512:1024] = last[8:].astype(BF16)
    stores[1].start()
    total = ga3[px, py // 2]
    for o in (1, 7, 2, 6, 3, 5, 4):
        remote(*ga_y(o)).wait_recv()
        total = total + ga6[o].astype(F32)
    mine = jnp.where(par == 0, total[:8], total[8:])
    for k in range(2):
        for h in range(2):
            rows = slice(8 * h, 8 * h + 8)
            lanes = 32 * (2 * k + h)
            gk = mine[:, lanes : lanes + 32]
            pa[k, rows, :], mao[k, rows, :], vao[k, rows, :] = adam(
                a[k, rows, :], ma[k, rows, :], va[k, rows, :], gk
            )
    for i in (2, 4, 5):
        stores[i].start()
    settle()
    y_send_wait(1)
    for store in stores:
        store.wait()


def hand_over(*refs):
    ins, outs, held, (in_sem, out_sem) = refs[:8], refs[8:16], refs[16:24], refs[24:]
    loads = [pltpu.make_async_copy(ins[i], held[i], in_sem.at[i]) for i in range(8)]
    stores = [pltpu.make_async_copy(held[i], outs[i], out_sem.at[i]) for i in range(8)]
    for load in loads:
        load.start()
    for load, store in zip(loads, stores):
        load.wait()
        store.start()
    for store in stores:
        store.wait()


def per_device(tok, cot, w, a, b, ma, va, mb, vb):
    a, ma, va = (jnp.swapaxes(t, 1, 2) for t in (a, ma, va))
    args = (tok, cot, w, a, b, ma, va, mb, vb)
    outs = tuple(jax.ShapeDtypeStruct(t.shape, t.dtype) for t in (cot, tok, a, b, a, a, b, b))
    vmem, dma = pltpu.VMEM, pltpu.SemaphoreType.DMA
    res = pl.pallas_call(
        kernel,
        out_shape=outs,
        in_specs=[pl.BlockSpec(memory_space=pl.ANY)] * 9,
        out_specs=[pl.BlockSpec(memory_space=pl.ANY)] * 8,
        scratch_shapes=[vmem(t.shape, t.dtype) for t in args + outs]
        + [
            vmem((NZ, NC, 2, 16, 640), BF16),
            vmem((8, 128), F32),
            vmem((32, 128), F32),
            vmem((NZ, NC, 32, 128), BF16),
            vmem((32, HID), F32),
            vmem((128, 2 * HID), BF16),
            vmem((2, 128, 1024), BF16),
            vmem((32, 1024), F32),
            vmem((128, 1024), BF16),
            vmem((2, NZ, 16, HID), F32),
            vmem((2, NZ, 16, HID), BF16),
            vmem((2, NZ, 16, HID), BF16),
            vmem((2, 5, 16, HID), BF16),
            vmem((2, 5, 16, HID), BF16),
            vmem((2, 2, 16, HID), BF16),
            vmem((2, 2, 16, HID), BF16),
            vmem((NC, NZ, 16, 128), BF16),
            vmem((ROWS, 16, 128), BF16),
            vmem((16, HID), F32),
            vmem((NC, NZ, 16, WIDTH[0]), BF16),
            vmem((NC, NZ, 16, WIDTH[1]), BF16),
            vmem((2, 128, 128), F32),
            vmem((2, NX, 4, 16, 512), F32),
            vmem((2, 3, 4, 16, 512), BF16),
            vmem((2, 3, 4, 16, 512), BF16),
            vmem((2, 4, 16, 512), BF16),
            vmem((NY, 16, 512), BF16),
            vmem((NX, 4, 16, 128), F32),
            vmem((3, 4, 16, 128), BF16),
            vmem((3, 4, 16, 128), BF16),
            vmem((4, 16, 128), BF16),
            vmem((NY, 16, 128), BF16),
            dma((9,)), dma((8,)),
            dma((32,)), dma((32,)),
            dma((NZ,)), dma((NZ,)),
            dma((2,)), dma((2,)),
            dma((10,)), dma((10,)),
            dma((4,)), dma((4,)),
            dma((ROWS,)), dma((ROWS,)),
            dma((16,)), dma((16,)),
            dma((16,)), dma((16,)),
            dma((6,)), dma((6,)),
            dma((8,)), dma((8,)),
            dma((3,)), dma((3,)),
            dma((8,)), dma((8,)),
        ],
        compiler_params=pltpu.CompilerParams(
            collective_id=0, has_side_effects=True, vmem_limit_bytes=60 * 1024 * 1024
        ),
    )(*args)
    hid, dx, pa, pb, mao, vao, mbo, vbo = pl.pallas_call(
        hand_over,
        out_shape=outs,
        in_specs=[pl.BlockSpec(memory_space=pl.ANY)] * 8,
        out_specs=[pl.BlockSpec(memory_space=pl.ANY)] * 8,
        scratch_shapes=[vmem(t.shape, t.dtype) for t in outs] + [dma((8,)), dma((8,))],
        compiler_params=pltpu.CompilerParams(vmem_limit_bytes=60 * 1024 * 1024),
    )(*res)
    pa, mao, vao = (jnp.swapaxes(t, 1, 2) for t in (pa, mao, vao))
    return hid, dx, pa, pb, mao, vao, mbo, vbo


def solution(mesh):
    placed = (
        P("col", "row"),
        P("row", "col"),
        P(None, "row", "col"),
        P(None, ("row", "col"), None),
        P(None, None, ("col", "row")),
        P(None, ("row", "col"), None),
        P(None, ("row", "col"), None),
        P(None, None, ("col", "row")),
        P(None, None, ("col", "row")),
    )
    return jax.shard_map(
        per_device,
        mesh=mesh,
        in_specs=placed,
        out_specs=(
            P("row", "col"),
            P("col", "row"),
            P(None, ("row", "col"), None),
            P(None, None, ("col", "row")),
            P(None, ("row", "col"), None),
            P(None, ("row", "col"), None),
            P(None, None, ("col", "row")),
            P(None, None, ("col", "row")),
        ),
        check_vma=False,
    )
```

```python
import jax
import jax.numpy as jnp
from jax import lax
from jax.experimental import pallas as pl
from jax.experimental.pallas import tpu as pltpu
from jax.sharding import PartitionSpec as P

F32 = jnp.float32
BF16 = jnp.bfloat16
MESH = pl.DeviceIdType.MESH
adapter_scale = 0.5
beta_one = 0.9
beta_two = 0.999
epsilon = 1e-08
learn_rate = 0.001
adam_step = 10.0

NX, NY, NZ, NC = 4, 8, 8, 2
ROWS, COLS = NZ * NC, NX * NY
HID = 896
WIDTH = (HID, HID + 128)
FAR_FIRST = (4, 3, 5, 2, 6, 1, 7)
NT = (((1,), (1,)), ((), ()))


def adam(param, moment, second, gradient):
    moment_new = beta_one * moment + (1.0 - beta_one) * gradient
    second_new = beta_two * second + (1.0 - beta_two) * gradient * gradient
    update = (
        moment_new
        / (1.0 - beta_one**adam_step)
        / (jnp.sqrt(second_new / (1.0 - beta_two**adam_step)) + epsilon)
    )
    return (param - learn_rate * update, moment_new, second_new)


def dot(a, b):
    return jnp.dot(a, b, preferred_element_type=F32)


def kernel(
    tok_h, cot_h, w_h, a_h, b_h, ma_h, va_h, mb_h, vb_h,
    hid_o, dx_o, pa_o, pb_o, mao_o, vao_o, mbo_o, vbo_o,
    tok, cot, w, a, b, ma, va, mb, vb,
    hid, dxv, pa, pb, mao, vao, mbo, vbo,
    tblk, aw, bw, bblk, bf, bb, x, af, at, yo, s1, r1, sa, ra, sb, rb, lows, lowr, hidf, d0, d1, fac,
    s3, s4, r3, s5, r5, ga3, ga4, gar, ga5, ga6,
    in_sem, out_sem, t_send, t_recv, b_send, b_recv, c_send, c_recv, a_send, a_recv, f_send, f_recv,
    l_send, l_recv, g_send, g_recv, p_send, p_recv, x_send, x_recv, y_send, y_recv, q_send, q_recv, k_send, k_recv,
):
    d = (d0, d1)
    row, col = lax.axis_index("row"), lax.axis_index("col")
    z, c = row // NC, row % NC
    px, py = col // NY, col % NY
    par = py % 2
    oc = 1 - c
    sgn = 1 - 2 * c

    def zc(off):
        return lax.rem(z + sgn * off + NZ, NZ)

    def at_z(off):
        return (zc(off) * NC + c, col)

    def at_y(off):
        return (row, px * NY + lax.rem(py + off, NY))

    def at_x(off):
        return (row, lax.rem(px + off, NX) * NY + py)

    def at_row(off):
        return (lax.rem(row + off, ROWS), col)

    partner = (z * NC + oc, col)

    def remote(src, dst, send, recv, to):
        return pltpu.make_async_remote_copy(
            src_ref=src, dst_ref=dst, send_sem=send, recv_sem=recv, device_id=to, device_id_type=MESH
        )

    sends = []

    def go(*copy):
        copy = remote(*copy)
        copy.start()
        sends.append(copy)

    def settle(most=1000):
        for copy in sends[:most]:
            copy.wait_send()
        del sends[:most]

    barrier = pltpu.get_barrier_semaphore()
    greet = [at_y(o) for o in FAR_FIRST] + [at_x(o) for o in (2, 1, 3)] + [at_row(o) for o in range(1, ROWS)]
    for peer in greet:
        pl.semaphore_signal(barrier, inc=1, device_id=peer, device_id_type=MESH)

    loads = [
        pltpu.make_async_copy(h, v, in_sem.at[i])
        for i, (h, v) in enumerate(
            [(tok_h, tok), (a_h, a), (b_h, b), (w_h, w), (cot_h, cot), (ma_h, ma), (va_h, va), (mb_h, mb), (vb_h, vb)]
        )
    ]
    for load in loads[:3]:
        load.start()
    outs = [(hid, hid_o), (dxv, dx_o), (pa, pa_o), (pb, pb_o), (mao, mao_o), (vao, vao_o), (mbo, mbo_o), (vbo, vbo_o)]
    stores = [pltpu.make_async_copy(v, h, out_sem.at[i]) for i, (v, h) in enumerate(outs)]

    for load in loads[3:]:
        load.start()

    def block(xx, yy):
        return tblk.at[2 * xx + yy // 4, (yy // 2) % 2, yy % 2]

    for load in loads[:2]:
        load.wait()
    t = tok[...].astype(F32)
    for k in range(2):
        for h in range(2):
            j = 2 * k + h
            aw[:, 32 * j : 32 * j + 32] = a[k, 8 * h : 8 * h + 8, :]
    own = block(px, py)
    own[:, 0:512] = jnp.concatenate([t[:, :512], t[:, 512:]], axis=0).astype(BF16)
    own[:, 512:640] = jnp.concatenate([aw[...], jnp.zeros((8, 128), F32)], axis=0).astype(BF16)
    pl.semaphore_wait(barrier, len(greet))

    def blk_at(xo, yy):
        return block(lax.rem(px - xo + NX, NX), lax.rem(py - yy + NY, NY))

    def t_y(o):
        return (own, own, t_send.at[o], t_recv.at[o], at_y(o))

    def t_x(yy, xo):
        blk, i = blk_at(0, yy), 7 + 3 * yy + xo
        return (blk, blk, t_send.at[i], t_recv.at[i], at_x(xo))

    def t_near(yy, xo):
        blk, i = blk_at(xo, 0), 7 + 3 * yy + xo
        return (blk, blk, t_send.at[i], t_recv.at[i], at_y(yy))

    far = [jnp.where(par == 0, e, o) for e, o in zip((2, 6, 4, 3, 5), (3, 5, 2, 6, 4))]
    for o in far:
        go(*t_y(o))
    for o in (2, 1, 3):
        go(*t_x(0, o))
    for o in (1, 7):
        go(*t_y(o))
    loads[2].wait()
    bw[...] = jnp.zeros((32, 128), F32)
    for k in range(2):
        bw[16 * k : 16 * k + 16, 0:56] = b[k]
    bblk[z, c] = bw[...].astype(BF16)

    def b_cross():
        return (bblk.at[z, c], bblk.at[z, c], b_send.at[0], b_recv.at[0], partner)

    def b_z(o):
        return (bblk.at[z], bblk.at[z], b_send.at[o], b_recv.at[o], at_z(o))

    go(*b_cross())

    def near(xo):
        remote(*t_x(0, xo)).wait_recv()
        go(*t_near(1, xo))
        go(*t_near(7, xo))

    def spread(i):
        remote(*t_y(far[i])).wait_recv()
        for o in (2, 1, 3):
            go(*t_x(far[i], o))

    near(1)
    near(3)
    spread(0)
    spread(1)
    near(2)
    for i in (2, 3, 4):
        spread(i)
    remote(*b_cross()).wait_recv()
    for o in FAR_FIRST:
        go(*b_z(o))

    def take(g):
        @pl.when(par == g)
        def _():
            for yy in (2, 6, 4):
                for o in (1, 3, 2):
                    remote(*t_x(yy, o)).wait_recv()

        @pl.when(par != g)
        def _():
            for yy in (1, 7):
                remote(*t_y(yy)).wait_recv()
            for yy in (1, 7, 3, 5):
                for o in (1, 3, 2):
                    remote(*t_x(yy, o)).wait_recv()

        for rel in range(2):
            u = tblk[:, oc if rel == 0 else c, g].astype(F32)
            x[g, 64 * rel : 64 * rel + 64, 0:512] = u[:, :8, :512].reshape(64, 512).astype(BF16)
            x[g, 64 * rel : 64 * rel + 64, 512:1024] = u[:, 8:, :512].reshape(64, 512).astype(BF16)

    def core_copy(g):
        return (s1.at[g], r1.at[g], c_send.at[g], c_recv.at[g], partner)

    def forward(g):
        src = x[g]
        gate, up = dot(src, w[0]), dot(src, w[1])
        other = [p[:64].reshape(NZ, 8, HID) for p in (gate, up)]
        s1[g] = jnp.concatenate(other, axis=1).astype(BF16)
        go(*core_copy(g))
        mine = [p[64:].reshape(NZ, 8, HID) for p in (gate, up)]
        yo[g] = jnp.concatenate(mine, axis=1)

    def sum_copy(g, i, to):
        return (sa.at[g, i], ra.at[g, i], a_send.at[5 * g + i], a_recv.at[5 * g + i], at_z(to))

    first = ((4, 2), (3, 1), (-3, -1), (1, 1), (-1, -1))

    def sum_first(g):
        remote(*core_copy(g)).wait_recv()
        yo[g] = yo[g] + r1[g].astype(F32)
        for i, (owner, to) in enumerate(first):
            sa[g, i] = yo[g, zc(owner)].astype(BF16)
            go(*sum_copy(g, i, to))

    def second_copy(g, i):
        return (sb.at[g, i], rb.at[g, i], f_send.at[2 * g + i], f_recv.at[2 * g + i], at_z((2, -2)[i]))

    def sum_second(g):
        remote(*sum_copy(g, 1, 1)).wait_recv()
        remote(*sum_copy(g, 0, 2)).wait_recv()
        sb[g, 0] = (yo[g, zc(2)] + ra[g, 0].astype(F32) + ra[g, 1].astype(F32)).astype(BF16)
        go(*second_copy(g, 0))
        remote(*sum_copy(g, 2, -1)).wait_recv()
        sb[g, 1] = (yo[g, zc(-2)] + ra[g, 2].astype(F32)).astype(BF16)
        go(*second_copy(g, 1))

    def low_copy(o):
        to = lax.rem(row + o, ROWS)
        rel = jnp.where(to % NC == c, 1, 0)
        return (lows.at[rel, to // NC], lowr.at[o], l_send.at[o], l_recv.at[o], (to, col))

    def low_sends():
        both = [
            lax.dot_general(x[g], at[...], NT, preferred_element_type=F32).reshape(NC, NZ, 8, 128) for g in range(2)
        ]
        lows[...] = jnp.concatenate(both, axis=2).astype(BF16)
        for o in range(1, ROWS):
            go(*low_copy(o))

    def low_total():
        total = lows[1, z].astype(F32)
        for o in range(1, ROWS):
            remote(*low_copy(o)).wait_recv()
            total = total + lowr[o].astype(F32)
        keep = lax.broadcasted_iota(jnp.int32, (16, 128), 1) < 32
        return jnp.where(keep, total, 0.0).astype(BF16)

    def pass_copy(g, off, to):
        blk = d[g].at[1, zc(-off)]
        i = 8 * g + (off + to) % 8
        return (blk, blk, g_send.at[i], g_recv.at[i], at_z(to))

    def cross(g, off):
        i = 8 * g + off % 8
        return (d[g].at[1, zc(-off)], d[g].at[0, zc(-off)], p_send.at[i], p_recv.at[i], partner)

    def activate(g, gate_low, up_low, low_half):
        for i in (3, 4):
            remote(*sum_copy(g, i, first[i][1])).wait_recv()
        for i in (0, 1):
            remote(*second_copy(g, i)).wait_recv()
        total = yo[g, z] + ra[g, 3].astype(F32) + ra[g, 4].astype(F32) + rb[g, 0].astype(F32) + rb[g, 1].astype(F32)
        gate = total[:8] + gate_low[8 * g : 8 * g + 8]
        up = total[8:] + up_low[8 * g : 8 * g + 8]
        sig = jax.nn.sigmoid(gate)
        silu = gate * sig
        grad = cot[...].astype(F32)[8 * g : 8 * g + 8]
        d_gate = grad * up * sig * (1.0 + gate * (1.0 - sig))
        d_up = grad * silu
        d[g][1, z, :, 0:HID] = jnp.concatenate([d_gate, d_up], axis=0).astype(BF16)
        if g == 1:
            d[g][1, z, :, HID:] = low_half
        for to in (2, 1, -2, -1):
            go(*pass_copy(g, 0, to))
        go(*cross(g, 0))
        hidf[8 * g : 8 * g + 8, :] = silu * up

    def pass_on(g):
        remote(*pass_copy(g, 0, 1)).wait_recv()
        go(*cross(g, 1))
        remote(*pass_copy(g, 0, -1)).wait_recv()
        go(*cross(g, -1))
        remote(*pass_copy(g, 0, 2)).wait_recv()
        go(*pass_copy(g, 2, 2))
        go(*pass_copy(g, 2, 1))
        remote(*pass_copy(g, 0, -2)).wait_recv()
        go(*pass_copy(g, -2, -1))
        go(*cross(g, 2))
        go(*cross(g, -2))

    def pass_last(g):
        remote(*pass_copy(g, 2, 1)).wait_recv()
        go(*cross(g, 3))
        remote(*pass_copy(g, -2, -1)).wait_recv()
        go(*cross(g, -3))
        remote(*pass_copy(g, 2, 2)).wait_recv()
        go(*cross(g, 4))

    def crossed(g):
        for off in (0, 1, -1, 2, -2, 3, -3, 4):
            remote(*cross(g, off)).wait_recv()

    def halves(g):
        v = d[g][...].astype(F32)
        return [v[:, :, 8 * k : 8 * k + 8, :HID].reshape(128, HID).astype(BF16) for k in range(2)]

    def x_copy(g, o):
        return (s4.at[g, o - 1], r3.at[g, o - 1], x_send.at[3 * g + o - 1], x_recv.at[3 * g + o - 1], at_x(o))

    def backward(g):
        dg, du = halves(g)
        f = lax.dot_general(dg, bb[:, :HID], NT, preferred_element_type=F32)
        f = adapter_scale * (f + lax.dot_general(du, bb[:, HID:], NT, preferred_element_type=F32))
        e = lax.dot_general(dg, w[0], NT, preferred_element_type=F32)
        e = e + lax.dot_general(du, w[1], NT, preferred_element_type=F32)
        e = e + dot(f.astype(BF16), at[...])
        fac[g] = f
        e6 = e.reshape(2, NX, 2, 8, 1024)
        for rel in range(2):
            cc = oc if rel == 0 else c
            for h in range(2):
                blk = e6[rel, :, h]
                s3[g, :, 2 * h + cc] = jnp.concatenate([blk[:, :, :512], blk[:, :, 512:]], axis=1)
        for o in (2, 1, 3):
            s4[g, o - 1] = s3[g, lax.rem(px + o, NX)].astype(BF16)
            go(*x_copy(g, o))

    def y_copy(g, j):
        o = jnp.where(par == g, (4, 2, 6, 0)[j], (3, 5, 1, 7)[j])
        to = lax.rem(py + o, NY)
        return o, (s5.at[g, to // 2], r5.at[o], y_send.at[g * 4 + j], y_recv.at[o], (row, px * NY + to))

    def x_finish(g):
        total = s3[g, px]
        for o in (1, 3, 2):
            remote(*x_copy(g, o)).wait_recv()
            total = total + r3[g, o - 1].astype(F32)
        s3[g, px] = total
        s5[g] = total.astype(BF16)
        for j in range(4):
            o, copy = y_copy(g, j)

            @pl.when(o != 0)
            def _():
                remote(*copy).start()

    def y_send_wait(g):
        for j in range(4):
            o, copy = y_copy(g, j)

            @pl.when(o != 0)
            def _():
                remote(*copy).wait_send()

    loads[3].wait()
    take(0)
    forward(0)

    sum_first(0)
    for o in FAR_FIRST:
        remote(*b_z(o)).wait_recv()
    for r in range(ROWS):
        bf[:, 56 * r : 56 * r + 56] = bblk[r // NC, r % NC].astype(F32)[:, 0:56]
    bfull = bf[...].astype(BF16)
    bb[...] = jnp.zeros((128, 2 * HID), BF16)
    bb[0:16, 0:HID] = bfull[0:16]
    bb[16:32, HID:] = bfull[16:32]
    at[...] = jnp.zeros((128, 1024), BF16)

    take(1)
    forward(1)

    lane = lax.broadcasted_iota(jnp.int32, (8, 128), 1) // 32

    def regroup(pieces, g):
        out = None
        for q in range(4):
            p = pieces[q]
            shift = (32 * (q - g[q])) % 128
            if shift:
                p = pltpu.roll(p, shift, 1)
            out = p if out is None else jnp.where(lane == q, p, out)
        return out

    v = tblk[:, :, :, :, 512:640].astype(F32).reshape(COLS, 16, 128)
    for tile in range(8):
        four = [v[4 * tile + q, :8] for q in range(4)]
        for j in range(4):
            af[8 * j : 8 * j + 8, 128 * tile : 128 * tile + 128] = regroup(four, (j,) * 4)
    at[0:32, :] = af[...].astype(BF16)
    low_sends()
    sum_first(1)
    sum_second(0)
    sum_second(1)
    loads[4].wait()
    low_half = low_total()
    gate_low = adapter_scale * dot(low_half, bb[:, :HID])
    up_low = adapter_scale * dot(low_half, bb[:, HID:])
    activate(0, gate_low, up_low, low_half)
    activate(1, gate_low, up_low, low_half)
    hid[...] = hidf[...].astype(BF16)
    stores[0].start()
    settle(60)
    pass_on(0)
    pass_on(1)
    pass_last(0)
    crossed(0)
    backward(0)
    af[...] = dot(fac[0].T[:32].astype(BF16), x[0])
    pass_last(1)
    crossed(1)
    backward(1)
    ga = af[...] + dot(fac[1].T[:32].astype(BF16), x[1])
    for tile in range(8):
        four = [ga[8 * j : 8 * j + 8, 128 * tile : 128 * tile + 128] for j in range(4)]
        for q in range(4):
            yy = 4 * (tile % 2) + q
            ga3[tile // 2, yy // 2, 8 * (yy % 2) : 8 * (yy % 2) + 8, :] = regroup(four, (q,) * 4)

    def ga_x(o):
        return (ga4.at[o - 1], gar.at[o - 1], q_send.at[o - 1], q_recv.at[o - 1], at_x(o))

    for o in (2, 1, 3):
        ga4[o - 1] = ga3[lax.rem(px + o, NX)].astype(BF16)
        go(*ga_x(o))
    x_finish(0)

    low_all = d1[:, :, :, HID:].astype(F32)
    gb = [None, None]
    for g in range(2):
        low_t = low_all[:, :, 8 * g : 8 * g + 8].reshape(128, 128).T[:32].astype(BF16)
        for k, h in enumerate(halves(g)):
            p = dot(low_t, h)[16 * k : 16 * k + 16]
            gb[k] = p if g == 0 else gb[k] + p
    for load in loads[5:]:
        load.wait()
    shift = lax.rem(HID - 56 * row, HID)
    for k in range(2):
        gk = pltpu.roll(adapter_scale * gb[k], shift, 1)[:, :56]
        pb[k], mbo[k], vbo[k] = adam(b[k], mb[k], vb[k], gk)
    for i in (3, 6, 7):
        stores[i].start()
    x_finish(1)
    total = ga3[px]
    for o in (1, 3, 2):
        remote(*ga_x(o)).wait_recv()
        total = total + gar[o - 1].astype(F32)
    ga3[px] = total
    ga5[...] = total.astype(BF16)

    def ga_y(o):
        to = lax.rem(py + o, NY)
        return (ga5.at[to // 2], ga6.at[o], k_send.at[o], k_recv.at[o], (row, px * NY + to))

    for o in FAR_FIRST:
        go(*ga_y(o))
    y_send_wait(0)
    last = s3[par, px, py // 2]
    for o in (1, 7, 2, 6, 3, 5, 4):
        remote(s5.at[0, 0], r5.at[o], y_send.at[0], y_recv.at[o], at_y(o)).wait_recv()
        last = last + r5[o].astype(F32)
    dxv[:, 0:512] = last[:8].astype(BF16)
    dxv[:, 512:1024] = last[8:].astype(BF16)
    stores[1].start()
    total = ga3[px, py // 2]
    for o in (1, 7, 2, 6, 3, 5, 4):
        remote(*ga_y(o)).wait_recv()
        total = total + ga6[o].astype(F32)
    mine = jnp.where(par == 0, total[:8], total[8:])
    for k in range(2):
        for h in range(2):
            rows = slice(8 * h, 8 * h + 8)
            lanes = 32 * (2 * k + h)
            gk = mine[:, lanes : lanes + 32]
            pa[k, rows, :], mao[k, rows, :], vao[k, rows, :] = adam(
                a[k, rows, :], ma[k, rows, :], va[k, rows, :], gk
            )
    for i in (2, 4, 5):
        stores[i].start()
    settle()
    y_send_wait(1)
    for store in stores:
        store.wait()


def hand_over(*refs):
    ins, outs, held, (in_sem, out_sem) = refs[:8], refs[8:16], refs[16:24], refs[24:]
    loads = [pltpu.make_async_copy(ins[i], held[i], in_sem.at[i]) for i in range(8)]
    stores = [pltpu.make_async_copy(held[i], outs[i], out_sem.at[i]) for i in range(8)]
    for load in loads:
        load.start()
    for load, store in zip(loads, stores):
        load.wait()
        store.start()
    for store in stores:
        store.wait()


def per_device(tok, cot, w, a, b, ma, va, mb, vb):
    a, ma, va = (jnp.swapaxes(t, 1, 2) for t in (a, ma, va))
    args = (tok, cot, w, a, b, ma, va, mb, vb)
    outs = tuple(jax.ShapeDtypeStruct(t.shape, t.dtype) for t in (cot, tok, a, b, a, a, b, b))
    vmem, dma = pltpu.VMEM, pltpu.SemaphoreType.DMA
    res = pl.pallas_call(
        kernel,
        out_shape=outs,
        in_specs=[pl.BlockSpec(memory_space=pl.ANY)] * 9,
        out_specs=[pl.BlockSpec(memory_space=pl.ANY)] * 8,
        scratch_shapes=[vmem(t.shape, t.dtype) for t in args + outs]
        + [
            vmem((NZ, NC, 2, 16, 640), BF16),
            vmem((8, 128), F32),
            vmem((32, 128), F32),
            vmem((NZ, NC, 32, 128), BF16),
            vmem((32, HID), F32),
            vmem((128, 2 * HID), BF16),
            vmem((2, 128, 1024), BF16),
            vmem((32, 1024), F32),
            vmem((128, 1024), BF16),
            vmem((2, NZ, 16, HID), F32),
            vmem((2, NZ, 16, HID), BF16),
            vmem((2, NZ, 16, HID), BF16),
            vmem((2, 5, 16, HID), BF16),
            vmem((2, 5, 16, HID), BF16),
            vmem((2, 2, 16, HID), BF16),
            vmem((2, 2, 16, HID), BF16),
            vmem((NC, NZ, 16, 128), BF16),
            vmem((ROWS, 16, 128), BF16),
            vmem((16, HID), F32),
            vmem((NC, NZ, 16, WIDTH[0]), BF16),
            vmem((NC, NZ, 16, WIDTH[1]), BF16),
            vmem((2, 128, 128), F32),
            vmem((2, NX, 4, 16, 512), F32),
            vmem((2, 3, 4, 16, 512), BF16),
            vmem((2, 3, 4, 16, 512), BF16),
            vmem((2, 4, 16, 512), BF16),
            vmem((NY, 16, 512), BF16),
            vmem((NX, 4, 16, 128), F32),
            vmem((3, 4, 16, 128), BF16),
            vmem((3, 4, 16, 128), BF16),
            vmem((4, 16, 128), BF16),
            vmem((NY, 16, 128), BF16),
            dma((9,)), dma((8,)),
            dma((32,)), dma((32,)),
            dma((NZ,)), dma((NZ,)),
            dma((2,)), dma((2,)),
            dma((10,)), dma((10,)),
            dma((4,)), dma((4,)),
            dma((ROWS,)), dma((ROWS,)),
            dma((16,)), dma((16,)),
            dma((16,)), dma((16,)),
            dma((6,)), dma((6,)),
            dma((8,)), dma((8,)),
            dma((3,)), dma((3,)),
            dma((8,)), dma((8,)),
        ],
        compiler_params=pltpu.CompilerParams(
            collective_id=0, has_side_effects=True, vmem_limit_bytes=60 * 1024 * 1024
        ),
    )(*args)
    hid, dx, pa, pb, mao, vao, mbo, vbo = pl.pallas_call(
        hand_over,
        out_shape=outs,
        in_specs=[pl.BlockSpec(memory_space=pl.ANY)] * 8,
        out_specs=[pl.BlockSpec(memory_space=pl.ANY)] * 8,
        scratch_shapes=[vmem(t.shape, t.dtype) for t in outs] + [dma((8,)), dma((8,))],
        compiler_params=pltpu.CompilerParams(vmem_limit_bytes=60 * 1024 * 1024),
    )(*res)
    pa, mao, vao = (jnp.swapaxes(t, 1, 2) for t in (pa, mao, vao))
    return hid, dx, pa, pb, mao, vao, mbo, vbo


def solution(mesh):
    placed = (
        P("col", "row"),
        P("row", "col"),
        P(None, "row", "col"),
        P(None, ("row", "col"), None),
        P(None, None, ("col", "row")),
        P(None, ("row", "col"), None),
        P(None, ("row", "col"), None),
        P(None, None, ("col", "row")),
        P(None, None, ("col", "row")),
    )
    return jax.shard_map(
        per_device,
        mesh=mesh,
        in_specs=placed,
        out_specs=(
            P("row", "col"),
            P("col", "row"),
            P(None, ("row", "col"), None),
            P(None, None, ("col", "row")),
            P(None, ("row", "col"), None),
            P(None, ("row", "col"), None),
            P(None, None, ("col", "row")),
            P(None, None, ("col", "row")),
        ),
        check_vma=False,
    )
```

```python
import jax
import jax.numpy as jnp
from jax import lax
from jax.experimental import pallas as pl
from jax.experimental.pallas import tpu as pltpu
from jax.sharding import PartitionSpec as P

F32 = jnp.float32
BF16 = jnp.bfloat16
MESH = pl.DeviceIdType.MESH
adapter_scale = 0.5
beta_one = 0.9
beta_two = 0.999
epsilon = 1e-08
learn_rate = 0.001
adam_step = 10.0

NX, NY, NZ, NC = 4, 8, 8, 2
ROWS, COLS = NZ * NC, NX * NY
HID = 896
WIDTH = (HID, HID + 128)
FAR_FIRST = (4, 3, 5, 2, 6, 1, 7)
NT = (((1,), (1,)), ((), ()))


def adam(param, moment, second, gradient):
    moment_new = beta_one * moment + (1.0 - beta_one) * gradient
    second_new = beta_two * second + (1.0 - beta_two) * gradient * gradient
    update = (
        moment_new
        / (1.0 - beta_one**adam_step)
        / (jnp.sqrt(second_new / (1.0 - beta_two**adam_step)) + epsilon)
    )
    return (param - learn_rate * update, moment_new, second_new)


def dot(a, b):
    return jnp.dot(a, b, preferred_element_type=F32)


def kernel(
    tok_h, cot_h, w_h, a_h, b_h, ma_h, va_h, mb_h, vb_h,
    hid_o, dx_o, pa_o, pb_o, mao_o, vao_o, mbo_o, vbo_o,
    tok, cot, w, a, b, ma, va, mb, vb,
    hid, dxv, pa, pb, mao, vao, mbo, vbo,
    tblk, aw, bw, bblk, bf, bb, x, af, at, yo, s1, r1, sa, ra, sb, rb, lows, lowr, hidf, d0, d1, fac,
    s3, s4, r3, s5, r5, ga3, ga4, gar, ga5, ga6,
    in_sem, out_sem, t_send, t_recv, b_send, b_recv, c_send, c_recv, a_send, a_recv, f_send, f_recv,
    l_send, l_recv, g_send, g_recv, p_send, p_recv, x_send, x_recv, y_send, y_recv, q_send, q_recv, k_send, k_recv,
):
    d = (d0, d1)
    row, col = lax.axis_index("row"), lax.axis_index("col")
    z, c = row // NC, row % NC
    px, py = col // NY, col % NY
    par = py % 2
    oc = 1 - c
    sgn = 1 - 2 * c

    def zc(off):
        return lax.rem(z + sgn * off + NZ, NZ)

    def at_z(off):
        return (zc(off) * NC + c, col)

    def at_y(off):
        return (row, px * NY + lax.rem(py + off, NY))

    def at_x(off):
        return (row, lax.rem(px + off, NX) * NY + py)

    partner = (z * NC + oc, col)

    def remote(src, dst, send, recv, to):
        return pltpu.make_async_remote_copy(
            src_ref=src, dst_ref=dst, send_sem=send, recv_sem=recv, device_id=to, device_id_type=MESH
        )

    sends = []

    def go(*copy):
        copy = remote(*copy)
        copy.start()
        sends.append(copy)

    def settle(most=1000):
        for copy in sends[:most]:
            copy.wait_send()
        del sends[:most]

    barrier = pltpu.get_barrier_semaphore()
    greet = [at_y(o) for o in FAR_FIRST] + [at_x(o) for o in (2, 1, 3)] + [at_z(o) for o in FAR_FIRST] + [partner]
    for peer in greet:
        pl.semaphore_signal(barrier, inc=1, device_id=peer, device_id_type=MESH)

    loads = [
        pltpu.make_async_copy(h, v, in_sem.at[i])
        for i, (h, v) in enumerate(
            [(tok_h, tok), (a_h, a), (b_h, b), (w_h, w), (cot_h, cot), (ma_h, ma), (va_h, va), (mb_h, mb), (vb_h, vb)]
        )
    ]
    for load in loads[:3]:
        load.start()
    outs = [(hid, hid_o), (dxv, dx_o), (pa, pa_o), (pb, pb_o), (mao, mao_o), (vao, vao_o), (mbo, mbo_o), (vbo, vbo_o)]
    stores = [pltpu.make_async_copy(v, h, out_sem.at[i]) for i, (v, h) in enumerate(outs)]

    for load in loads[3:]:
        load.start()

    def block(xx, yy):
        return tblk.at[2 * xx + yy // 4, (yy // 2) % 2, yy % 2]

    for load in loads[:2]:
        load.wait()
    t = tok[...].astype(F32)
    for k in range(2):
        for h in range(2):
            j = 2 * k + h
            aw[:, 32 * j : 32 * j + 32] = a[k, 8 * h : 8 * h + 8, :]
    own = block(px, py)
    own[:, 0:512] = jnp.concatenate([t[:, :512], t[:, 512:]], axis=0).astype(BF16)
    own[:, 512:640] = jnp.concatenate([aw[...], jnp.zeros((8, 128), F32)], axis=0).astype(BF16)
    pl.semaphore_wait(barrier, len(greet))

    def blk_at(xo, yy):
        return block(lax.rem(px - xo + NX, NX), lax.rem(py - yy + NY, NY))

    def t_y(o):
        return (own, own, t_send.at[o], t_recv.at[o], at_y(o))

    def t_x(yy, xo):
        blk, i = blk_at(0, yy), 7 + 3 * yy + xo
        return (blk, blk, t_send.at[i], t_recv.at[i], at_x(xo))

    def t_near(yy, xo):
        blk, i = blk_at(xo, 0), 7 + 3 * yy + xo
        return (blk, blk, t_send.at[i], t_recv.at[i], at_y(yy))

    far = [jnp.where(par == 0, e, o) for e, o in zip((2, 6, 4, 3, 5), (3, 5, 2, 6, 4))]
    for o in far:
        go(*t_y(o))
    for o in (2, 1, 3):
        go(*t_x(0, o))
    for o in (1, 7):
        go(*t_y(o))
    loads[2].wait()
    bw[...] = jnp.zeros((32, 128), F32)
    for k in range(2):
        bw[16 * k : 16 * k + 16, 0:56] = b[k]
    bblk[z, c] = bw[...].astype(BF16)

    def b_cross():
        return (bblk.at[z, c], bblk.at[z, c], b_send.at[0], b_recv.at[0], partner)

    def b_z(o):
        return (bblk.at[z], bblk.at[z], b_send.at[o], b_recv.at[o], at_z(o))

    go(*b_cross())

    def near(xo):
        remote(*t_x(0, xo)).wait_recv()
        go(*t_near(1, xo))
        go(*t_near(7, xo))

    def spread(i):
        remote(*t_y(far[i])).wait_recv()
        for o in (2, 1, 3):
            go(*t_x(far[i], o))

    near(1)
    near(3)
    spread(0)
    spread(1)
    near(2)
    for i in (2, 3, 4):
        spread(i)
    remote(*b_cross()).wait_recv()
    for o in FAR_FIRST:
        go(*b_z(o))

    def take(g):
        @pl.when(par == g)
        def _():
            for yy in (2, 6, 4):
                for o in (1, 3, 2):
                    remote(*t_x(yy, o)).wait_recv()

        @pl.when(par != g)
        def _():
            for yy in (1, 7):
                remote(*t_y(yy)).wait_recv()
            for yy in (1, 7, 3, 5):
                for o in (1, 3, 2):
                    remote(*t_x(yy, o)).wait_recv()

        for rel in range(2):
            u = tblk[:, oc if rel == 0 else c, g].astype(F32)
            x[g, 64 * rel : 64 * rel + 64, 0:512] = u[:, :8, :512].reshape(64, 512).astype(BF16)
            x[g, 64 * rel : 64 * rel + 64, 512:1024] = u[:, 8:, :512].reshape(64, 512).astype(BF16)

    def core_copy(g):
        return (s1.at[g], r1.at[g], c_send.at[g], c_recv.at[g], partner)

    def forward(g):
        src = x[g]
        gate, up = dot(src, w[0]), dot(src, w[1])
        other = [p[:64].reshape(NZ, 8, HID) for p in (gate, up)]
        s1[g] = jnp.concatenate(other, axis=1).astype(BF16)
        go(*core_copy(g))
        mine = [p[64:].reshape(NZ, 8, HID) for p in (gate, up)]
        yo[g] = jnp.concatenate(mine, axis=1)

    def sum_copy(g, i, to):
        return (sa.at[g, i], ra.at[g, i], a_send.at[5 * g + i], a_recv.at[5 * g + i], at_z(to))

    first = ((4, 2), (3, 1), (-3, -1), (1, 1), (-1, -1))

    def sum_first(g):
        remote(*core_copy(g)).wait_recv()
        yo[g] = yo[g] + r1[g].astype(F32)
        for i, (owner, to) in enumerate(first):
            sa[g, i] = yo[g, zc(owner)].astype(BF16)
            go(*sum_copy(g, i, to))

    def second_copy(g, i):
        return (sb.at[g, i], rb.at[g, i], f_send.at[2 * g + i], f_recv.at[2 * g + i], at_z((2, -2)[i]))

    def sum_second(g):
        remote(*sum_copy(g, 1, 1)).wait_recv()
        remote(*sum_copy(g, 0, 2)).wait_recv()
        sb[g, 0] = (yo[g, zc(2)] + ra[g, 0].astype(F32) + ra[g, 1].astype(F32)).astype(BF16)
        go(*second_copy(g, 0))
        remote(*sum_copy(g, 2, -1)).wait_recv()
        sb[g, 1] = (yo[g, zc(-2)] + ra[g, 2].astype(F32)).astype(BF16)
        go(*second_copy(g, 1))

    def low_cross():
        return (lows.at[0], lowr.at[0], l_send.at[0], l_recv.at[0], partner)

    def low_z(o):
        to = lax.rem(z + o, NZ)
        return (lows.at[1, to], lowr.at[1, o], l_send.at[o], l_recv.at[o], (to * NC + c, col))

    def low_sends():
        both = [
            lax.dot_general(x[g], at[...], NT, preferred_element_type=F32).reshape(NC, NZ, 8, 128) for g in range(2)
        ]
        lows[...] = jnp.concatenate(both, axis=2).astype(BF16)
        go(*low_cross())

    def low_next():
        remote(*low_cross()).wait_recv()
        lows[1] = (lows[1].astype(F32) + lowr[0].astype(F32)).astype(BF16)
        for o in FAR_FIRST:
            go(*low_z(o))

    def low_total():
        total = lows[1, z].astype(F32)
        for o in FAR_FIRST:
            remote(*low_z(o)).wait_recv()
            total = total + lowr[1, o].astype(F32)
        keep = lax.broadcasted_iota(jnp.int32, (16, 128), 1) < 32
        return jnp.where(keep, total, 0.0).astype(BF16)

    def pass_copy(g, off, to):
        blk = d[g].at[1, zc(-off)]
        i = 8 * g + (off + to) % 8
        return (blk, blk, g_send.at[i], g_recv.at[i], at_z(to))

    def cross(g, off):
        i = 8 * g + off % 8
        return (d[g].at[1, zc(-off)], d[g].at[0, zc(-off)], p_send.at[i], p_recv.at[i], partner)

    def activate(g, gate_low, up_low, low_half):
        for i in (3, 4):
            remote(*sum_copy(g, i, first[i][1])).wait_recv()
        for i in (0, 1):
            remote(*second_copy(g, i)).wait_recv()
        total = yo[g, z] + ra[g, 3].astype(F32) + ra[g, 4].astype(F32) + rb[g, 0].astype(F32) + rb[g, 1].astype(F32)
        gate = total[:8] + gate_low[8 * g : 8 * g + 8]
        up = total[8:] + up_low[8 * g : 8 * g + 8]
        sig = jax.nn.sigmoid(gate)
        silu = gate * sig
        grad = cot[...].astype(F32)[8 * g : 8 * g + 8]
        d_gate = grad * up * sig * (1.0 + gate * (1.0 - sig))
        d_up = grad * silu
        d[g][1, z, :, 0:HID] = jnp.concatenate([d_gate, d_up], axis=0).astype(BF16)
        if g == 1:
            d[g][1, z, :, HID:] = low_half
        for to in (2, 1, -2, -1):
            go(*pass_copy(g, 0, to))
        go(*cross(g, 0))
        hidf[8 * g : 8 * g + 8, :] = silu * up

    def pass_on(g):
        remote(*pass_copy(g, 0, 1)).wait_recv()
        go(*cross(g, 1))
        remote(*pass_copy(g, 0, -1)).wait_recv()
        go(*cross(g, -1))
        remote(*pass_copy(g, 0, 2)).wait_recv()
        go(*pass_copy(g, 2, 2))
        go(*pass_copy(g, 2, 1))
        remote(*pass_copy(g, 0, -2)).wait_recv()
        go(*pass_copy(g, -2, -1))
        go(*cross(g, 2))
        go(*cross(g, -2))

    def pass_last(g):
        remote(*pass_copy(g, 2, 1)).wait_recv()
        go(*cross(g, 3))
        remote(*pass_copy(g, -2, -1)).wait_recv()
        go(*cross(g, -3))
        remote(*pass_copy(g, 2, 2)).wait_recv()
        go(*cross(g, 4))

    def crossed(g):
        for off in (0, 1, -1, 2, -2, 3, -3, 4):
            remote(*cross(g, off)).wait_recv()

    def halves(g):
        v = d[g][...].astype(F32)
        return [v[:, :, 8 * k : 8 * k + 8, :HID].reshape(128, HID).astype(BF16) for k in range(2)]

    def x_copy(g, o):
        return (s4.at[g, o - 1], r3.at[g, o - 1], x_send.at[3 * g + o - 1], x_recv.at[3 * g + o - 1], at_x(o))

    def backward(g):
        dg, du = halves(g)
        f = lax.dot_general(dg, bb[:, :HID], NT, preferred_element_type=F32)
        f = adapter_scale * (f + lax.dot_general(du, bb[:, HID:], NT, preferred_element_type=F32))
        e = lax.dot_general(dg, w[0], NT, preferred_element_type=F32)
        e = e + lax.dot_general(du, w[1], NT, preferred_element_type=F32)
        e = e + dot(f.astype(BF16), at[...])
        fac[g] = f
        e6 = e.reshape(2, NX, 2, 8, 1024)
        for rel in range(2):
            cc = oc if rel == 0 else c
            for h in range(2):
                blk = e6[rel, :, h]
                s3[g, :, 2 * h + cc] = jnp.concatenate([blk[:, :, :512], blk[:, :, 512:]], axis=1)
        for o in (2, 1, 3):
            s4[g, o - 1] = s3[g, lax.rem(px + o, NX)].astype(BF16)
            go(*x_copy(g, o))

    def y_copy(g, j):
        o = jnp.where(par == g, (4, 2, 6, 0)[j], (3, 5, 1, 7)[j])
        to = lax.rem(py + o, NY)
        return o, (s5.at[g, to // 2], r5.at[o], y_send.at[g * 4 + j], y_recv.at[o], (row, px * NY + to))

    def x_finish(g):
        total = s3[g, px]
        for o in (1, 3, 2):
            remote(*x_copy(g, o)).wait_recv()
            total = total + r3[g, o - 1].astype(F32)
        s3[g, px] = total
        s5[g] = total.astype(BF16)
        for j in range(4):
            o, copy = y_copy(g, j)

            @pl.when(o != 0)
            def _():
                remote(*copy).start()

    def y_send_wait(g):
        for j in range(4):
            o, copy = y_copy(g, j)

            @pl.when(o != 0)
            def _():
                remote(*copy).wait_send()

    loads[3].wait()
    take(0)
    forward(0)

    sum_first(0)
    for o in FAR_FIRST:
        remote(*b_z(o)).wait_recv()
    for r in range(ROWS):
        bf[:, 56 * r : 56 * r + 56] = bblk[r // NC, r % NC].astype(F32)[:, 0:56]
    bfull = bf[...].astype(BF16)
    bb[...] = jnp.zeros((128, 2 * HID), BF16)
    bb[0:16, 0:HID] = bfull[0:16]
    bb[16:32, HID:] = bfull[16:32]
    at[...] = jnp.zeros((128, 1024), BF16)

    take(1)
    forward(1)

    lane = lax.broadcasted_iota(jnp.int32, (8, 128), 1) // 32

    def regroup(pieces, g):
        out = None
        for q in range(4):
            p = pieces[q]
            shift = (32 * (q - g[q])) % 128
            if shift:
                p = pltpu.roll(p, shift, 1)
            out = p if out is None else jnp.where(lane == q, p, out)
        return out

    v = tblk[:, :, :, :, 512:640].astype(F32).reshape(COLS, 16, 128)
    for tile in range(8):
        four = [v[4 * tile + q, :8] for q in range(4)]
        for j in range(4):
            af[8 * j : 8 * j + 8, 128 * tile : 128 * tile + 128] = regroup(four, (j,) * 4)
    at[0:32, :] = af[...].astype(BF16)
    low_sends()
    sum_first(1)
    low_next()
    sum_second(0)
    sum_second(1)
    loads[4].wait()
    low_half = low_total()
    gate_low = adapter_scale * dot(low_half, bb[:, :HID])
    up_low = adapter_scale * dot(low_half, bb[:, HID:])
    activate(0, gate_low, up_low, low_half)
    activate(1, gate_low, up_low, low_half)
    hid[...] = hidf[...].astype(BF16)
    stores[0].start()
    settle(60)
    pass_on(0)
    pass_on(1)
    pass_last(0)
    crossed(0)
    backward(0)
    af[...] = dot(fac[0].T[:32].astype(BF16), x[0])
    pass_last(1)
    crossed(1)
    backward(1)
    ga = af[...] + dot(fac[1].T[:32].astype(BF16), x[1])
    for tile in range(8):
        four = [ga[8 * j : 8 * j + 8, 128 * tile : 128 * tile + 128] for j in range(4)]
        for q in range(4):
            yy = 4 * (tile % 2) + q
            ga3[tile // 2, yy // 2, 8 * (yy % 2) : 8 * (yy % 2) + 8, :] = regroup(four, (q,) * 4)

    def ga_x(o):
        return (ga4.at[o - 1], gar.at[o - 1], q_send.at[o - 1], q_recv.at[o - 1], at_x(o))

    for o in (2, 1, 3):
        ga4[o - 1] = ga3[lax.rem(px + o, NX)].astype(BF16)
        go(*ga_x(o))
    x_finish(0)

    low_all = d1[:, :, :, HID:].astype(F32)
    gb = [None, None]
    for g in range(2):
        low_t = low_all[:, :, 8 * g : 8 * g + 8].reshape(128, 128).T[:32].astype(BF16)
        for k, h in enumerate(halves(g)):
            p = dot(low_t, h)[16 * k : 16 * k + 16]
            gb[k] = p if g == 0 else gb[k] + p
    for load in loads[5:]:
        load.wait()
    shift = lax.rem(HID - 56 * row, HID)
    for k in range(2):
        gk = pltpu.roll(adapter_scale * gb[k], shift, 1)[:, :56]
        pb[k], mbo[k], vbo[k] = adam(b[k], mb[k], vb[k], gk)
    for i in (3, 6, 7):
        stores[i].start()
    x_finish(1)
    total = ga3[px]
    for o in (1, 3, 2):
        remote(*ga_x(o)).wait_recv()
        total = total + gar[o - 1].astype(F32)
    ga3[px] = total
    ga5[...] = total.astype(BF16)

    def ga_y(o):
        to = lax.rem(py + o, NY)
        return (ga5.at[to // 2], ga6.at[o], k_send.at[o], k_recv.at[o], (row, px * NY + to))

    for o in FAR_FIRST:
        go(*ga_y(o))
    y_send_wait(0)
    last = s3[par, px, py // 2]
    for o in (1, 7, 2, 6, 3, 5, 4):
        remote(s5.at[0, 0], r5.at[o], y_send.at[0], y_recv.at[o], at_y(o)).wait_recv()
        last = last + r5[o].astype(F32)
    dxv[:, 0:512] = last[:8].astype(BF16)
    dxv[:, 512:1024] = last[8:].astype(BF16)
    stores[1].start()
    total = ga3[px, py // 2]
    for o in (1, 7, 2, 6, 3, 5, 4):
        remote(*ga_y(o)).wait_recv()
        total = total + ga6[o].astype(F32)
    mine = jnp.where(par == 0, total[:8], total[8:])
    for k in range(2):
        for h in range(2):
            rows = slice(8 * h, 8 * h + 8)
            lanes = 32 * (2 * k + h)
            gk = mine[:, lanes : lanes + 32]
            pa[k, rows, :], mao[k, rows, :], vao[k, rows, :] = adam(
                a[k, rows, :], ma[k, rows, :], va[k, rows, :], gk
            )
    for i in (2, 4, 5):
        stores[i].start()
    settle()
    y_send_wait(1)
    for store in stores:
        store.wait()


def hand_over(*refs):
    ins, outs, held, (in_sem, out_sem) = refs[:8], refs[8:16], refs[16:24], refs[24:]
    loads = [pltpu.make_async_copy(ins[i], held[i], in_sem.at[i]) for i in range(8)]
    stores = [pltpu.make_async_copy(held[i], outs[i], out_sem.at[i]) for i in range(8)]
    for load in loads:
        load.start()
    for load, store in zip(loads, stores):
        load.wait()
        store.start()
    for store in stores:
        store.wait()


def per_device(tok, cot, w, a, b, ma, va, mb, vb):
    a, ma, va = (jnp.swapaxes(t, 1, 2) for t in (a, ma, va))
    args = (tok, cot, w, a, b, ma, va, mb, vb)
    outs = tuple(jax.ShapeDtypeStruct(t.shape, t.dtype) for t in (cot, tok, a, b, a, a, b, b))
    vmem, dma = pltpu.VMEM, pltpu.SemaphoreType.DMA
    res = pl.pallas_call(
        kernel,
        out_shape=outs,
        in_specs=[pl.BlockSpec(memory_space=pl.ANY)] * 9,
        out_specs=[pl.BlockSpec(memory_space=pl.ANY)] * 8,
        scratch_shapes=[vmem(t.shape, t.dtype) for t in args + outs]
        + [
            vmem((NZ, NC, 2, 16, 640), BF16),
            vmem((8, 128), F32),
            vmem((32, 128), F32),
            vmem((NZ, NC, 32, 128), BF16),
            vmem((32, HID), F32),
            vmem((128, 2 * HID), BF16),
            vmem((2, 128, 1024), BF16),
            vmem((32, 1024), F32),
            vmem((128, 1024), BF16),
            vmem((2, NZ, 16, HID), F32),
            vmem((2, NZ, 16, HID), BF16),
            vmem((2, NZ, 16, HID), BF16),
            vmem((2, 5, 16, HID), BF16),
            vmem((2, 5, 16, HID), BF16),
            vmem((2, 2, 16, HID), BF16),
            vmem((2, 2, 16, HID), BF16),
            vmem((NC, NZ, 16, 128), BF16),
            vmem((NC, NZ, 16, 128), BF16),
            vmem((16, HID), F32),
            vmem((NC, NZ, 16, WIDTH[0]), BF16),
            vmem((NC, NZ, 16, WIDTH[1]), BF16),
            vmem((2, 128, 128), F32),
            vmem((2, NX, 4, 16, 512), F32),
            vmem((2, 3, 4, 16, 512), BF16),
            vmem((2, 3, 4, 16, 512), BF16),
            vmem((2, 4, 16, 512), BF16),
            vmem((NY, 16, 512), BF16),
            vmem((NX, 4, 16, 128), F32),
            vmem((3, 4, 16, 128), BF16),
            vmem((3, 4, 16, 128), BF16),
            vmem((4, 16, 128), BF16),
            vmem((NY, 16, 128), BF16),
            dma((9,)), dma((8,)),
            dma((32,)), dma((32,)),
            dma((NZ,)), dma((NZ,)),
            dma((2,)), dma((2,)),
            dma((10,)), dma((10,)),
            dma((4,)), dma((4,)),
            dma((ROWS,)), dma((ROWS,)),
            dma((16,)), dma((16,)),
            dma((16,)), dma((16,)),
            dma((6,)), dma((6,)),
            dma((8,)), dma((8,)),
            dma((3,)), dma((3,)),
            dma((8,)), dma((8,)),
        ],
        compiler_params=pltpu.CompilerParams(
            collective_id=0, has_side_effects=True, vmem_limit_bytes=60 * 1024 * 1024
        ),
    )(*args)
    hid, dx, pa, pb, mao, vao, mbo, vbo = pl.pallas_call(
        hand_over,
        out_shape=outs,
        in_specs=[pl.BlockSpec(memory_space=pl.ANY)] * 8,
        out_specs=[pl.BlockSpec(memory_space=pl.ANY)] * 8,
        scratch_shapes=[vmem(t.shape, t.dtype) for t in outs] + [dma((8,)), dma((8,))],
        compiler_params=pltpu.CompilerParams(vmem_limit_bytes=60 * 1024 * 1024),
    )(*res)
    pa, mao, vao = (jnp.swapaxes(t, 1, 2) for t in (pa, mao, vao))
    return hid, dx, pa, pb, mao, vao, mbo, vbo


def solution(mesh):
    placed = (
        P("col", "row"),
        P("row", "col"),
        P(None, "row", "col"),
        P(None, ("row", "col"), None),
        P(None, None, ("col", "row")),
        P(None, ("row", "col"), None),
        P(None, ("row", "col"), None),
        P(None, None, ("col", "row")),
        P(None, None, ("col", "row")),
    )
    return jax.shard_map(
        per_device,
        mesh=mesh,
        in_specs=placed,
        out_specs=(
            P("row", "col"),
            P("col", "row"),
            P(None, ("row", "col"), None),
            P(None, None, ("col", "row")),
            P(None, ("row", "col"), None),
            P(None, ("row", "col"), None),
            P(None, None, ("col", "row")),
            P(None, None, ("col", "row")),
        ),
        check_vma=False,
    )
```
